128 devices in a mesh: phase: 8 (over z_hi, x), slab: 8 (over y, core), angle: 2 (over z_lo).
Axes of the slice: x: 4, y: 4, z: 4 (z_hi: 2, z_lo: 2; z = z_hi * 2 + z_lo), core: 2. Of those that a mesh axis runs over, the one named last changes fastest.
Arguments:
- measured: bfloat16 [8, 24, 272, 128], P('phase', 'angle'), may hold values from -6 to 6
- angles: int32 [8, 24], P('phase', 'angle'), may hold values from 0 to 639
- counts: int32 [8], replicated, may hold values from 10 to 24, as said below
- bands: int32 [8], replicated, may hold values from 0 to 232, as said below
- zfoot: bfloat16 [256, 40], P('slab'), may hold values from 0.049804688 to 0.5
Outputs:
- solution: float32 [8, 256, 16384], P('phase', 'slab')
- residual: float32 [8, 24, 320, 128], P('phase', 'angle', 'slab')
The draws below stay inside these ranges and needn't reach their ends.
Inputs may be any that keep to these rules, and one draw needn't show every extreme that they name: `counts`: every value lies between 10 and 24; some phase has exactly 24 and some exactly the least. bands[s] lies between s * 32 and s * 32 + 2 * 4; bands[0] = 0 and the last slab's band ends at row 272.
All inputs are finite; a program needn't handle non-finite values.
Results may differ from the reference program's by a relative error of at most 0.0033.
The reference program's roundings to bfloat16 on the way (of `weights`, `lines` and `part`) count: a program that leaves them out, or rounds other values in their place, can miss the bound.
Values may be sent and summed in bfloat16 or wider, within the bound.
A program may use at most 64 MiB of HBM per device.

```python
import math
import jax
import jax.numpy as jnp
from jax import lax

GRID = 128
DETECTOR_COLUMNS = 128
CZ = 32
MARG = 4
ANGLE_SLOT_COUNT = 24
NVIEW = 640
ITERS = 2
PHASE_COUNT = 8
SLAB_COUNT = 8
NZ = 256
CELLS = 16384
BAND_ROW_COUNT = 40
DROWS = 272


def draw_counts(key, part):
    key = jax.random.fold_in(key, 11)
    first, second = jax.random.split(key)
    lowest = ANGLE_SLOT_COUNT * 3 // 7
    values = jax.random.randint(first, (PHASE_COUNT,), lowest, ANGLE_SLOT_COUNT + 1)
    order = jax.random.permutation(second, PHASE_COUNT)
    values = values.at[order[0]].set(ANGLE_SLOT_COUNT).at[order[1]].set(lowest)
    return values.astype(jnp.int32)


def draw_bands(key, part):
    key = jax.random.fold_in(key, 23)
    shifts = jax.random.randint(key, (SLAB_COUNT,), 0, 2 * MARG + 1)
    shifts = shifts.at[0].set(0).at[SLAB_COUNT - 1].set(2 * MARG)
    return (jnp.arange(SLAB_COUNT, dtype=jnp.int32) * CZ + shifts).astype(jnp.int32)


def plant(result, rng, least, largest):
    longest = result.shape.index(max(result.shape))
    spots = []
    for shift in (0, 1):
        where = [jax.random.randint(jax.random.fold_in(rng, axis), (), 0, length) for axis, length in enumerate(result.shape)]
        where[longest] = (where[longest] + shift) % result.shape[longest]
        spots.append(tuple(where))
    return result.at[spots[0]].set(least).at[spots[1]].set(largest)


def levels(key, shape, cuts, low, largest):
    loudness, own = 1.0, jax.random.fold_in(key, 6)
    for axis_at, blocks in cuts:
        steps = jnp.exp(jax.random.uniform(jax.random.fold_in(own, axis_at), (blocks,), jnp.float32, low / len(cuts), largest / len(cuts)))
        loudness = loudness * jnp.repeat(steps, shape[axis_at] // blocks).reshape([-1 if axis == axis_at else 1 for axis in range(len(shape))])
    return loudness


def normal_values(rng, dims, scale, limit, shards=(), held_as=jnp.bfloat16):
    factor_of = levels(rng, dims, shards, -0.22, 0.18) if shards else 1.0
    entries = jax.random.normal(rng, dims, jnp.float32) * scale * factor_of
    return jnp.minimum(jnp.maximum(entries, -limit), limit).astype(held_as)


def setup_inputs(seed: int = 0) -> dict:
    streams_of = jax.random.split(jax.random.key(seed), 6)
    measured = normal_values(streams_of[0], (PHASE_COUNT, ANGLE_SLOT_COUNT, DROWS, DETECTOR_COLUMNS), 1.0, 6.0, ((0, 8), (1, 2)))
    angles = plant(jax.random.randint(streams_of[1], (PHASE_COUNT, ANGLE_SLOT_COUNT), 0, NVIEW), jax.random.fold_in(streams_of[1], 1), 0, NVIEW - 1).astype(jnp.int32)
    counts = draw_counts(jax.random.fold_in(streams_of[5], 71), 0)
    bands = draw_bands(jax.random.fold_in(streams_of[5], 71), 0)
    zfoot = jnp.clip(jnp.exp(math.log(0.5) - 2.306499 * jax.random.uniform(streams_of[4], (NZ, BAND_ROW_COUNT), jnp.float32) ** levels(streams_of[4], (NZ, BAND_ROW_COUNT), ((0, 8),), -0.2, 0.2)), 0.049804688, 0.5).astype(jnp.bfloat16)
    return {"measured": measured, "angles": angles, "counts": counts, "bands": bands, "zfoot": zfoot}


def footprints(theta, alive):
    cell = jnp.arange(GRID * GRID, dtype=jnp.int32)
    cross = (cell // GRID).astype(jnp.float32) + 0.5 - GRID / 2
    along = (cell % GRID).astype(jnp.float32) + 0.5 - GRID / 2
    shadow = cross[None, None, :] * jnp.cos(theta)[:, None, None] + along[None, None, :] * jnp.sin(theta)[:, None, None]
    centre = jnp.arange(DETECTOR_COLUMNS, dtype=jnp.int32).astype(jnp.float32) + 0.5 - DETECTOR_COLUMNS / 2
    weight = jnp.maximum(0.0, 1.0 - jnp.abs(shadow - centre[None, :, None]))
    return (weight * (alive[:, None, None] / math.sqrt(GRID))).astype(jnp.bfloat16)

def penalty(volume):
    return 2.0 * volume - jnp.roll(volume, 1, 0) - jnp.roll(volume, -1, 0)

def reference(measured, angles, counts, bands, zfoot):
    high = lax.Precision.HIGHEST
    slots = jnp.arange(ANGLE_SLOT_COUNT, dtype=jnp.int32)
    active_mask = (slots[None, :] < counts[:, None]).astype(jnp.float32)
    thetas = angles.astype(jnp.float32) * jnp.float32(math.pi / NVIEW)
    rows = jnp.arange(BAND_ROW_COUNT, dtype=jnp.int32)
    slot_index = (bands[:, None] + rows[None, :]).astype(jnp.int32)
    measured_band_rows = jnp.take(measured, slot_index.reshape(-1), axis=2).reshape(PHASE_COUNT, ANGLE_SLOT_COUNT, SLAB_COUNT, BAND_ROW_COUNT, DETECTOR_COLUMNS)
    prev_start = jnp.concatenate([bands[:1], bands[:-1]])
    owner = ((jnp.arange(SLAB_COUNT, dtype=jnp.int32)[:, None] == 0) | (slot_index >= prev_start[:, None] + BAND_ROW_COUNT)).astype(jnp.float32)
    place = (slot_index[:, :, None, None] == slot_index[None, None, :, :]).astype(jnp.float32)
    foot = zfoot.reshape(SLAB_COUNT, CZ, BAND_ROW_COUNT).astype(jnp.float32)
    blocks = ANGLE_SLOT_COUNT // 4
    th_blocks = thetas.reshape(PHASE_COUNT, blocks, 4)
    lv_blocks = active_mask.reshape(PHASE_COUNT, blocks, 4)

    def forward(volume):
        flat = volume.astype(jnp.bfloat16)

        def one_phase(trio):
            th_p, lv_p, vol_p = trio

            def one_block(pair):
                weights = footprints(pair[0], pair[1])
                lines = jnp.einsum('auc,zc->azu', weights.astype(jnp.float32), vol_p.astype(jnp.float32), precision=high).astype(jnp.bfloat16)
                lines = lines.reshape(4, SLAB_COUNT, CZ, DETECTOR_COLUMNS)
                return jnp.einsum('szv,aszu->asvu', foot, lines.astype(jnp.float32), precision=high).astype(jnp.bfloat16)
            part = lax.map(one_block, (th_p, lv_p)).reshape(ANGLE_SLOT_COUNT, SLAB_COUNT, BAND_ROW_COUNT, DETECTOR_COLUMNS)
            return jnp.einsum('sitk,atku->asiu', place, part.astype(jnp.float32), precision=high)
        return lax.map(one_phase, (th_blocks, lv_blocks, flat))

    def backproject(residual_block):
        rb = residual_block.astype(jnp.bfloat16).reshape(PHASE_COUNT, blocks, 4, SLAB_COUNT, BAND_ROW_COUNT, DETECTOR_COLUMNS)

        def one_phase(trio):
            th_p, lv_p, r_p = trio

            def add_block(total, item):
                weights = footprints(item[0], item[1])
                spread = jnp.einsum('szv,asvu->aszu', foot, item[2].astype(jnp.float32), precision=high).astype(jnp.bfloat16)
                spread = spread.reshape(4, NZ, DETECTOR_COLUMNS)
                return (total + jnp.einsum('auc,azu->zc', weights.astype(jnp.float32), spread.astype(jnp.float32), precision=high), None)
            total, _ = lax.scan(add_block, jnp.zeros((NZ, CELLS), jnp.float32), (th_p, lv_p, r_p))
            return total
        return lax.map(one_phase, (th_blocks, lv_blocks, rb))
    residual_block = active_mask[:, :, None, None, None] * measured_band_rows.astype(jnp.float32)
    solution = jnp.zeros((PHASE_COUNT, NZ, CELLS), jnp.float32)
    grad = backproject(residual_block)
    gamma = jnp.sum(grad * grad)
    direction = grad
    for step in range(ITERS):
        image = forward(direction)
        data_sum = jnp.sum(owner[None, None, :, :, None] * image * image)
        diff = direction - jnp.roll(direction, 1, 0)
        reg_sum = jnp.sum(diff * diff)
        alpha = gamma / (data_sum + reg_sum)
        solution = solution + alpha * direction
        residual_block = residual_block - alpha * image
        if step + 1 < ITERS:
            grad = backproject(residual_block) - penalty(solution)
            fresh = jnp.sum(grad * grad)
            direction = grad + fresh / gamma * direction
            gamma = fresh
    return (solution, residual_block.reshape(PHASE_COUNT, ANGLE_SLOT_COUNT, SLAB_COUNT * BAND_ROW_COUNT, DETECTOR_COLUMNS))
```

```python
import functools
import math

import jax
import jax.numpy as jnp
from jax import lax
from jax.experimental import pallas as pl
from jax.experimental.pallas import tpu as pltpu
from jax.sharding import PartitionSpec as P

GRID = 128
NVIEW = 640
CZ = 32
BAND = 40
SLOTS = 24
OWN = 12
SIDE = 16
WIN = 32
KS = 8
JS = 4
BLK = SLOTS // 4
SCALE = 1.0 / math.sqrt(GRID)
ROWS = KS * 256
PAD = 96
F32 = jnp.float32
BF16 = jnp.bfloat16


def fdot(a, b):
    return jnp.dot(a, b, preferred_element_type=F32)


def remote(src, dst, send, recv, **where):
    return pltpu.make_async_remote_copy(
        src_ref=src,
        dst_ref=dst,
        send_sem=send,
        recv_sem=recv,
        device_id=where,
        device_id_type=pl.DeviceIdType.MESH,
    )


def kernel(
    meas, u0, r0s, live, r0l, csl, ssh, lc, zft, zf4, sel4, sel0, own,
    out_d, out_g, out_c, out_r,
    wt, w, rbuf, sk, srep, mbuf, res, d0, pd0, g1, d0b, g1b, nbr, nbg, par_d, par_g,
    lown, lsend, lrecv, part, img, edge, halo, red1, red2, red3,
    s_m, s_vs, s_vr, s_ls, s_lr, s_es, s_er, s_rs, s_rr,
):
    ph, sl, an = (lax.axis_index(n) for n in ("phase", "slab", "angle"))
    barrier = pltpu.get_barrier_semaphore()
    mesh_id = pl.DeviceIdType.MESH
    for d in range(1, 8):
        pl.semaphore_signal(barrier, 1, device_id={"slab": lax.rem(sl + d, 8)}, device_id_type=mesh_id)
        pl.semaphore_signal(barrier, 1, device_id={"phase": lax.rem(ph + d, 8)}, device_id_type=mesh_id)
    pl.semaphore_signal(barrier, 1, device_id={"angle": 1 - an}, device_id_type=mesh_id)
    pl.semaphore_wait(barrier, 15)

    band_rows = meas.at[0, :, pl.ds(pl.multiple_of(sl * CZ, CZ), 48), :]
    local = pltpu.make_async_copy(band_rows, mbuf.at[0], s_m.at[0])
    local.start()
    away = remote(band_rows, mbuf.at[1], s_m.at[1], s_m.at[2], angle=1 - an)
    away.start()

    lane_group = lax.broadcasted_iota(jnp.int32, (1, 128), 1) // 32

    def clear(e, _):
        rbuf[pl.ds(e * 16, PAD // 8)] = jnp.zeros((PAD // 8, 8, 128), F32)
        return 0

    lax.fori_loop(0, KS * 16 + 1, clear, 0)

    def make_wt(k, _):
        for j in range(JS):
            base = r0l[pl.ds(k, 1), j * 768 : (j + 1) * 768]
            for g in range(SIDE):
                x = (base + csl[...] * float(g)) + ssh[...]
                value = jnp.maximum(0.0, SCALE - jnp.abs(x)).astype(BF16)
                wt[k, g * SIDE : (g + 1) * SIDE, j * 768 : (j + 1) * 768] = value
        return 0

    lax.fori_loop(0, KS, make_wt, 0)

    columns = lax.broadcasted_iota(jnp.int32, (WIN, 1), 0).astype(F32) * SCALE

    def make_w(t, _):
        b, k = t // KS, lax.rem(t, KS)
        for i in range(4):
            row = lc[pl.ds(b * 4 + i, 1), :]
            for j in range(JS):
                x = (row + r0s[k * 96 + j * SLOTS + b * 4 + i]) - columns
                value = jnp.maximum(0.0, SCALE - jnp.abs(x)).astype(BF16)
                w[b, k, (i * JS + j) * WIN : (i * JS + j + 1) * WIN, :] = value
        return 0

    lax.fori_loop(0, BLK * KS, make_w, 0)

    local.wait()
    away.wait()

    def first(b, _):
        half, third = b // 3, lax.rem(b, 3)
        rows = mbuf[half, pl.ds(third * 4, 4)].reshape(192, 128)
        res[b] = fdot(sel0[...], rows)
        return 0

    lax.fori_loop(0, BLK, first, 0)

    def spread(src):
        def body(b, _):
            for i in range(4):
                rt = src(b)[i * BAND : (i + 1) * BAND, :].T.astype(BF16)
                sp = fdot(rt, zft[...]).astype(BF16).astype(F32)
                srep[pl.ds((b * 4 + i) * 16, 16)] = sp.reshape(16, 8, 128)
            return 0

        lax.fori_loop(0, BLK, body, 0)

    def back(lo, hi, put):
        def body(k, _):
            for j in range(JS):
                for a in range(SLOTS):
                    x = srep[pl.ds(a * 16 + u0[k * 96 + j * SLOTS + a], WIN // 8)].reshape(WIN, 128)
                    spot = j * 768 + a * WIN
                    sk[spot : spot + WIN, :] = jnp.where(lane_group == j, x, 0.0).astype(BF16)
            put(pl.ds(pl.multiple_of(k * 256, 256), 256), fdot(wt[k], sk[...]))
            return 0

        lax.fori_loop(lo, hi, body, 0)

    def lines_copy(n, b):
        there = lax.rem(b + 3, BLK)
        return remote(lsend.at[n, b], lrecv.at[n, there], s_ls.at[n, b], s_lr.at[n, there], angle=1 - an)

    def up_copy(n, b):
        return remote(
            edge.at[n, b, pl.ds(0, 64)], halo.at[n, b, pl.ds(0, 64)], s_es.at[n, b, 0], s_er.at[n, b, 0],
            slab=lax.rem(sl + 1, 8),
        )

    def down_copy(n, b):
        return remote(
            edge.at[n, b, pl.ds(64, 64)], halo.at[n, b, pl.ds(64, 64)], s_es.at[n, b, 1], s_er.at[n, b, 1],
            slab=lax.rem(sl + 7, 8),
        )

    def project(vol, n):
        def body(b, _):
            def multiply(k, _):
                o = fdot(w[b, k], vol[pl.ds(pl.multiple_of(k * 256, 256), 256), :])
                for e in range(16):
                    rbuf[pl.ds((k * 16 + e) * 16 + PAD // 8, WIN // 8)] = o[e * WIN : (e + 1) * WIN].reshape(-1, 8, 128)
                return 0

            lax.fori_loop(0, KS, multiply, 0)
            packed = None
            for i in range(4):
                total = None
                for j in range(JS):
                    acc = None
                    for k in range(KS):
                        shift = u0[k * 96 + j * SLOTS + b * 4 + i]
                        x = rbuf[pl.ds((k * 16 + i * JS + j) * 16 + PAD // 8 - shift, 16)]
                        acc = x if acc is None else acc + x
                    acc = acc.reshape(128, 128)
                    total = acc if total is None else jnp.where(lane_group == j, acc, total)
                total = total + pltpu.roll(total, 64, 1)
                total = total + pltpu.roll(total, 32, 1)
                packed = total if packed is None else jnp.where(lane_group == i, total, packed)
            lown[b] = packed
            lsend[n, b] = packed.astype(BF16)
            lines_copy(n, b).start()
            return 0

        lax.fori_loop(0, BLK, body, 0)

    def partials(n):
        def body(t, _):
            b = lax.rem(t + 3, BLK)
            lines_copy(n, lax.rem(b + 3, BLK)).wait_recv()
            lines = (lown[b] + lrecv[n, b].astype(F32)).astype(BF16)
            pp = lax.dot_general(zf4[...], lines, (((1,), (1,)), ((), ())), preferred_element_type=F32).astype(BF16)
            part[b] = pp[:160].astype(F32)
            edge[n, b] = pp[160:]
            up_copy(n, b).start()
            down_copy(n, b).start()
            return 0

        lax.fori_loop(0, BLK, body, 0)

        def join(t, _):
            b = lax.rem(t + 3, BLK)
            up_copy(n, b).wait_recv()
            down_copy(n, b).wait_recv()
            img[n, b] = part[b] + fdot(sel4[...], halo[n, b])
            return 0

        lax.fori_loop(0, BLK, join, 0)

    def fold(x):
        return x.reshape(-1, 8, 128).sum(0)

    def stage_of(stage):
        return ((red1, "slab", sl, 8), (red2, "phase", ph, 8), (red3, "angle", an, 2))[stage]

    def stage_copies(n, stage, arriving):
        buf, axis, me, size = stage_of(stage)
        copies = []
        for d in range(1, size):
            to = lax.rem(me + d, size)
            slot = lax.rem(me + size - d, size) if arriving else me
            base = (0, 8, 16)[stage]
            place = buf.at[n, slot]
            copies.append(remote(place, place, s_rs.at[n, base + d], s_rr.at[n, base + slot], **{axis: to}))
        return copies

    def send_stage(n, stage, value):
        buf, _, me, _ = stage_of(stage)
        buf[n, me] = value
        for copy in stage_copies(n, stage, False):
            copy.start()

    def take_stage(n, stage):
        buf, _, _, size = stage_of(stage)
        for copy in stage_copies(n, stage, True):
            copy.wait_recv()
        total = buf[n, 0]
        for i in range(1, size):
            total = total + buf[n, i]
        return total

    spread(lambda b: res[b])

    def put_first(at, o):
        d0[at, :] = o
        d0b[at, :] = o.astype(BF16)

    back(0, KS, put_first)
    up_d = remote(d0b, nbr.at[0], s_vs.at[0], s_vr.at[0], phase=lax.rem(ph + 1, 8))
    down_d = remote(d0b, nbr.at[1], s_vs.at[1], s_vr.at[1], phase=lax.rem(ph + 7, 8))
    pair_d = remote(d0b, par_d, s_vs.at[2], s_vr.at[2], angle=1 - an)
    up_d.start()
    down_d.start()
    project(d0b, 0)
    partials(0)
    pair_d.start()

    spread(lambda b: img[0, b])
    up_d.wait_recv()
    down_d.wait_recv()
    zero = jnp.zeros((8, 128), F32)

    def first_sums(k, carry):
        gam, den = carry
        at = pl.ds(pl.multiple_of(k * 256, 256), 256)
        v = d0[at, :]
        p = 2.0 * v - nbr[0, at, :].astype(F32) - nbr[1, at, :].astype(F32)
        pd0[at, :] = p
        return gam + fold(v * v), den + fold(v * p)

    gam, den = lax.fori_loop(0, KS, first_sums, (zero, zero))

    def image_sums(b, den):
        im = img[0, b]
        return den + fold(own[...] * im * im)

    den = lax.fori_loop(0, 3, image_sums, den)

    def put_second(at, o):
        g1[at, :] = o

    send_stage(0, 0, jnp.concatenate([gam, den, zero], 0))
    back(0, 2, put_second)
    send_stage(0, 1, take_stage(0, 0))
    back(2, 5, put_second)
    send_stage(0, 2, take_stage(0, 1))
    back(5, KS, put_second)
    sums = take_stage(0, 2)
    gamma0 = jnp.sum(sums[0:8], axis=(0, 1), keepdims=True)
    den0 = jnp.sum(sums[8:16], axis=(0, 1), keepdims=True)
    alpha0 = gamma0 / den0

    def second_grad(k, carry):
        gam, cross = carry
        at = pl.ds(pl.multiple_of(k * 256, 256), 256)
        p = pd0[at, :]
        v = d0[at, :] - alpha0 * (g1[at, :] + p)
        g1[at, :] = v
        g1b[at, :] = v.astype(BF16)
        return gam + fold(v * v), cross + fold(v * p)

    gam, cross = lax.fori_loop(0, KS, second_grad, (zero, zero))
    half = ROWS // 2
    up_g = remote(g1b.at[pl.ds(0, half)], nbg.at[pl.ds(0, half)], s_vs.at[3], s_vr.at[3], phase=lax.rem(ph + 1, 8))
    down_g = remote(
        g1b.at[pl.ds(half, half)], nbg.at[pl.ds(half, half)], s_vs.at[4], s_vr.at[4], phase=lax.rem(ph + 7, 8)
    )
    pair_g = remote(g1b, par_g, s_vs.at[5], s_vr.at[5], angle=1 - an)
    up_g.start()
    down_g.start()
    project(g1b, 1)
    partials(1)
    pair_g.start()
    up_g.wait_recv()
    down_g.wait_recv()

    def second_sums(k, acc):
        at = pl.ds(pl.multiple_of(k * 256, 256), 256)
        return acc + fold(g1[at, :] * nbg[at, :].astype(F32))

    lag = lax.fori_loop(0, KS, second_sums, zero)

    def image_sums2(b, carry):
        den, cross = carry
        im = img[1, b]
        wi = own[...] * im
        return den + fold(wi * im), cross + fold(wi * img[0, b])

    den, cross = lax.fori_loop(0, 3, image_sums2, (2.0 * gam - 2.0 * lag, cross))
    send_stage(1, 0, jnp.concatenate([gam, den, cross], 0))

    def turn(src, dst, side):
        def body(g, _):
            cells = jnp.concatenate(
                [src[pl.ds(pl.multiple_of(k * 256 + g * SIDE, SIDE), SIDE), :].astype(F32) for k in range(KS)], 0
            ).T.astype(BF16)
            for j in range(JS):
                column = pl.multiple_of((side * 64 + j * SIDE + g) * 128, 128)
                dst[:, pl.ds(column, 128)] = cells[j * 32 : (j + 1) * 32]
            return 0

        lax.fori_loop(0, SIDE, body, 0)

    turn(d0b, out_d, an)
    send_stage(1, 1, take_stage(1, 0))
    pair_d.wait_recv()
    turn(par_d, out_d, 1 - an)
    send_stage(1, 2, take_stage(1, 1))
    turn(g1b, out_g, an)
    sums = take_stage(1, 2)
    gamma1 = jnp.sum(sums[0:8], axis=(0, 1), keepdims=True)
    den1 = jnp.sum(sums[8:16], axis=(0, 1), keepdims=True)
    cross1 = jnp.sum(sums[16:24], axis=(0, 1), keepdims=True)
    beta = gamma1 / gamma0
    alpha1 = gamma1 / (den1 + 2.0 * beta * cross1 + beta * beta * den0)
    c0 = alpha0 + alpha1 * beta
    out_c[...] = jnp.concatenate(
        [jnp.broadcast_to(c0, (8, 128)), jnp.broadcast_to(alpha1, (8, 128))], 0
    )

    def last(b, _):
        for i in range(4):
            at = slice(i * BAND, (i + 1) * BAND)
            out_r[b * 4 + i] = (
                live[b * 4 + i] * res[b, at, :] - c0 * img[0, b, at, :] - alpha1 * img[1, b, at, :]
            )
        return 0

    lax.fori_loop(0, 3, last, 0)
    pair_g.wait_recv()
    turn(par_g, out_g, 1 - an)

    for copy in (up_d, down_d, pair_d, up_g, down_g, pair_g):
        copy.wait_send()
    for n in range(2):

        def sent(b, _):
            lines_copy(n, b).wait_send()
            up_copy(n, b).wait_send()
            down_copy(n, b).wait_send()
            return 0

        lax.fori_loop(0, BLK, sent, 0)
        for stage in range(3):
            for copy in stage_copies(n, stage, False):
                copy.wait_send()


def tables(angles, counts, bands, zfoot):
    ph, sl, an = (lax.axis_index(n) for n in ("phase", "slab", "angle"))
    other = lax.ppermute(angles, "angle", [(0, 1), (1, 0)])
    slot = jnp.arange(OWN, dtype=jnp.int32)
    ids = jnp.concatenate([an * OWN + slot, (1 - an) * OWN + slot])
    alive = ids < lax.dynamic_index_in_dim(counts, ph, keepdims=False)
    theta = jnp.concatenate([angles[0], other[0]]).astype(F32) * jnp.float32(math.pi / NVIEW)
    cos, sin = jnp.cos(theta), jnp.sin(theta)
    left = (an * 64 + jnp.arange(JS) * SIDE).astype(F32) + 0.5 - GRID / 2
    low = (jnp.arange(KS) * SIDE).astype(F32) + 0.5 - GRID / 2
    corner = left[None, :, None] * cos + low[:, None, None] * sin
    least = corner + (SIDE - 1) * (jnp.minimum(cos, 0.0) + jnp.minimum(sin, 0.0))
    first = jnp.floor(least + (GRID / 2 - 1.5 - 1e-3)).astype(jnp.int32) + 1
    u0 = jnp.clip((first // 8) * 8, 0, GRID - WIN)
    r0 = jnp.where(alive, SCALE * (corner - u0.astype(F32) + (GRID / 2 - 0.5)), 1e3)
    win = jnp.arange(WIN, dtype=jnp.int32).astype(F32) * SCALE
    r0l = (r0[..., None] - win).reshape(KS, JS * SLOTS * WIN)
    csl = jnp.repeat(SCALE * cos, WIN)[None, :]
    side = jnp.arange(SIDE, dtype=jnp.int32).astype(F32)
    ssh = side[:, None] * jnp.repeat(SCALE * sin, WIN)[None, :]
    lc = SCALE * (side[None, :, None] * cos[:, None, None] + side[None, None, :] * sin[:, None, None])
    lc = lc.reshape(SLOTS, 256)

    zt = zfoot.T
    zft = jnp.tile(zt, (1, 4))
    eye = jnp.eye(4, dtype=BF16)
    diagonal = lambda m: (eye[:, None, :, None] * m[None, :, None, :]).reshape(4 * m.shape[0], 4 * m.shape[1])
    zf4 = jnp.concatenate([diagonal(zt), diagonal(zt[BAND - 16 :]), diagonal(zt[:16])], 0)
    start = lax.dynamic_index_in_dim(bands, sl, keepdims=False)
    below = lax.dynamic_index_in_dim(bands, jnp.maximum(sl - 1, 0), keepdims=False)
    above = lax.dynamic_index_in_dim(bands, jnp.minimum(sl + 1, 7), keepdims=False)
    rows = start + jnp.arange(BAND, dtype=jnp.int32)
    sixteen = jnp.arange(16, dtype=jnp.int32)
    from_lower = (rows[:, None] == below + BAND - 16 + sixteen) & (sl > 0)
    from_upper = (rows[:, None] == above + sixteen) & (sl < 7)
    sel4 = jnp.concatenate([diagonal(from_lower.astype(BF16)), diagonal(from_upper.astype(BF16))], 1)
    sel0 = diagonal((rows[:, None] == sl * CZ + jnp.arange(48, dtype=jnp.int32)).astype(BF16))
    own = jnp.where(sl == 0, 1.0, (rows >= below + BAND).astype(F32))
    own = jnp.broadcast_to(jnp.tile(own, 4)[:, None], (4 * BAND, 128))
    return (
        (u0 // 8).reshape(-1), r0.reshape(-1), alive.astype(F32), r0l, csl, ssh, lc, zft, zf4, sel4, sel0, own,
    )


def per_device(measured, angles, counts, bands, zfoot):
    made = tables(angles, counts, bands, zfoot)
    vmem, smem = pl.BlockSpec(memory_space=pltpu.VMEM), pl.BlockSpec(memory_space=pltpu.SMEM)
    volume16, volume32 = pltpu.VMEM((ROWS, 128), BF16), pltpu.VMEM((ROWS, 128), F32)
    out_d, out_g, out_c, out_r = pl.pallas_call(
        kernel,
        out_shape=(
            jax.ShapeDtypeStruct((CZ, GRID * GRID), BF16),
            jax.ShapeDtypeStruct((CZ, GRID * GRID), BF16),
            jax.ShapeDtypeStruct((16, 128), F32),
            jax.ShapeDtypeStruct((OWN, BAND, 128), F32),
        ),
        in_specs=[pl.BlockSpec(memory_space=pl.ANY)] + [smem] * 3 + [vmem] * 9,
        out_specs=(vmem,) * 4,
        scratch_shapes=[
            pltpu.VMEM((KS, 256, JS * SLOTS * WIN), BF16),
            pltpu.VMEM((BLK, KS, 16 * WIN, 256), BF16),
            pltpu.VMEM((KS * 256 + PAD // 8, 8, 128), F32),
            pltpu.VMEM((JS * SLOTS * WIN, 128), BF16),
            pltpu.VMEM((SLOTS * 16, 8, 128), F32),
            pltpu.VMEM((2, OWN, 48, 128), BF16),
            pltpu.VMEM((BLK, 4 * BAND, 128), F32),
            volume32, volume32, volume32, volume16, volume16,
            pltpu.VMEM((2, ROWS, 128), BF16),
            volume16, volume16, volume16,
            pltpu.VMEM((BLK, 128, 128), F32),
            pltpu.VMEM((2, BLK, 128, 128), BF16),
            pltpu.VMEM((2, BLK, 128, 128), BF16),
            pltpu.VMEM((BLK, 4 * BAND, 128), F32),
            pltpu.VMEM((2, BLK, 4 * BAND, 128), F32),
            pltpu.VMEM((2, BLK, 128, 128), BF16),
            pltpu.VMEM((2, BLK, 128, 128), BF16),
            pltpu.VMEM((2, 8, 24, 128), F32),
            pltpu.VMEM((2, 8, 24, 128), F32),
            pltpu.VMEM((2, 2, 24, 128), F32),
            pltpu.SemaphoreType.DMA((3,)),
            pltpu.SemaphoreType.DMA((6,)),
            pltpu.SemaphoreType.DMA((6,)),
            pltpu.SemaphoreType.DMA((2, BLK)),
            pltpu.SemaphoreType.DMA((2, BLK)),
            pltpu.SemaphoreType.DMA((2, BLK, 2)),
            pltpu.SemaphoreType.DMA((2, BLK, 2)),
            pltpu.SemaphoreType.DMA((2, 18)),
            pltpu.SemaphoreType.DMA((2, 18)),
        ],
        compiler_params=pltpu.CompilerParams(
            collective_id=0, has_side_effects=True, vmem_limit_bytes=60 * 1024 * 1024
        ),
    )(measured, *made)
    result = out_c[0, 0] * out_d.astype(F32) + out_c[8, 0] * out_g.astype(F32)
    return result[None], out_r[None]


def solution(mesh):
    placed = (P("phase", "angle", None, None), P("phase", "angle"), P(), P(), P("slab", None))
    return jax.shard_map(
        per_device,
        mesh=mesh,
        in_specs=placed,
        out_specs=(P("phase", "slab", None), P("phase", "angle", "slab", None)),
        check_vma=False,
    )
```

```python
import functools
import math

import jax
import jax.numpy as jnp
from jax import lax
from jax.experimental import pallas as pl
from jax.experimental.pallas import tpu as pltpu
from jax.sharding import PartitionSpec as P

GRID = 128
NVIEW = 640
CZ = 32
BAND = 40
SLOTS = 24
OWN = 12
SIDE = 16
WIN = 32
KS = 8
JS = 4
BLK = SLOTS // 4
SCALE = 1.0 / math.sqrt(GRID)
ROWS = KS * 256
PAD = 96
F32 = jnp.float32
BF16 = jnp.bfloat16


def fdot(a, b):
    return jnp.dot(a, b, preferred_element_type=F32)


def remote(src, dst, send, recv, **where):
    return pltpu.make_async_remote_copy(
        src_ref=src,
        dst_ref=dst,
        send_sem=send,
        recv_sem=recv,
        device_id=where,
        device_id_type=pl.DeviceIdType.MESH,
    )


def kernel(
    meas, angles, zfoot, counts, bands,
    out_d, out_g, out_c, out_r,
    ang, ints, floats, u0, r0s, r0l, csl, ssh, zft, zf4, sel4, sel0, own,
    wt, w, rbuf, rbuf2, sk, srep, mbuf, res, d0, pd0, g1, d0b, g1b, nbr, nbg, par_d, par_g,
    lown, lsend, lrecv, part, img, edge, halo, red1, red2, red3,
    s_a, s_m, s_vs, s_vr, s_ls, s_lr, s_es, s_er, s_rs, s_rr,
):
    ph, sl, an = (lax.axis_index(n) for n in ("phase", "slab", "angle"))
    barrier = pltpu.get_barrier_semaphore()
    mesh_id = pl.DeviceIdType.MESH
    for d in range(1, 8):
        pl.semaphore_signal(barrier, 1, device_id={"slab": lax.rem(sl + d, 8)}, device_id_type=mesh_id)
        pl.semaphore_signal(barrier, 1, device_id={"phase": lax.rem(ph + d, 8)}, device_id_type=mesh_id)
    pl.semaphore_signal(barrier, 1, device_id={"angle": 1 - an}, device_id_type=mesh_id)
    pl.semaphore_wait(barrier, 15)

    ang[0] = jnp.pad(angles[...], ((0, 7), (0, 128 - OWN)))
    angles_out = remote(ang.at[0], ang.at[1], s_a.at[0], s_a.at[1], angle=1 - an)
    angles_out.start()
    band_rows = meas.at[0, :, pl.ds(pl.multiple_of(sl * CZ, CZ), 48), :]
    local = pltpu.make_async_copy(band_rows, mbuf.at[0], s_m.at[0])
    local.start()
    away = remote(band_rows, mbuf.at[1], s_m.at[1], s_m.at[2], angle=1 - an)
    away.start()

    lane = lax.broadcasted_iota(jnp.int32, (1, 128), 1)
    lane_group = lane // 32

    def clear(e, _):
        rbuf[pl.ds(e * 16, PAD // 8)] = jnp.zeros((PAD // 8, 8, 128), F32)
        rbuf2[pl.ds(e * 16, PAD // 8)] = jnp.zeros((PAD // 8, 8, 128), F32)
        return 0

    lax.fori_loop(0, KS * 16 + 1, clear, 0)

    zt = zfoot[...].astype(F32).T
    zt = jnp.concatenate([zt] * 4, 1)
    zft[...] = zt.astype(BF16)
    groups = [jnp.where(lane_group == i, zt, 0.0) for i in range(4)]
    zf4[...] = jnp.concatenate(groups + [m[BAND - 16 :] for m in groups] + [m[:16] for m in groups], 0).astype(BF16)
    start = bands[sl]
    below, above = bands[jnp.maximum(sl - 1, 0)], bands[jnp.minimum(sl + 1, 7)]
    row = start + lax.broadcasted_iota(jnp.int32, (BAND, 1), 0)
    sixteenth = lane - (lane // 16) * 16
    other_row = jnp.where(lane < 64, below + BAND - 16, above) + sixteenth
    there = jnp.where(lane < 64, sl, 7 - sl) > 0
    slot4 = (lane // 16) - 4 * (lane // 64)
    sel4[...] = jnp.concatenate(
        [((row == other_row) & (there & (slot4 == i))).astype(F32) for i in range(4)], 0
    ).astype(BF16)
    wide = lax.broadcasted_iota(jnp.int32, (1, 192), 1)
    sel0[...] = jnp.concatenate(
        [(row - sl * CZ == wide - 48 * i).astype(F32) for i in range(4)], 0
    ).astype(BF16)
    mine = ((row >= below + BAND) | (sl == 0)).astype(F32)
    own[...] = jnp.concatenate([jnp.broadcast_to(mine, (BAND, 128))] * 4, 0)

    angles_out.wait()
    both = jnp.where(lane < OWN, ang[0], pltpu.roll(ang[1], OWN, 1)).astype(F32)
    slot_of = lax.broadcasted_iota(jnp.int32, (128, SLOTS * WIN), 0)
    lane_of = lax.broadcasted_iota(jnp.int32, (128, SLOTS * WIN), 1) // WIN
    one_hot = (slot_of == lane_of).astype(F32)
    expanded = jnp.dot(both, one_hot, precision=lax.Precision.HIGHEST, preferred_element_type=F32)
    count = counts[ph]

    def meet(angle, slot, left, low):
        theta = angle * F32(math.pi / NVIEW)
        cos, sin = jnp.cos(theta), jnp.sin(theta)
        ident = jnp.where(slot < OWN, an * OWN + slot, (1 - an) * OWN + slot - OWN)
        corner = left * cos + low * sin
        least = corner + (SIDE - 1) * (jnp.minimum(cos, 0.0) + jnp.minimum(sin, 0.0))
        first = jnp.floor(least + (GRID / 2 - 1.5 - 1e-3)) + 1.0
        eighth = jnp.clip(jnp.floor(first * 0.125), 0.0, float((GRID - WIN) // 8))
        base = SCALE * (corner - eighth * 8.0 + (GRID / 2 - 0.5))
        return cos, sin, eighth, jnp.where(ident < count, base, 1e3)

    def centre(i):
        return i.astype(F32) + (0.5 - GRID / 2)

    block = lax.broadcasted_iota(jnp.int32, (KS * JS, 1), 0)
    along = block // JS
    cos, sin, eighth, base = meet(
        both[0:1], lane, centre(an * 64 + (block - along * JS) * SIDE), centre(along * SIDE)
    )
    ints[...] = jnp.clip(eighth.astype(jnp.int32), 0, (GRID - WIN) // 8)
    floats[0 : KS * JS, :] = base
    floats[KS * JS : KS * JS + 8, :] = jnp.concatenate(
        [jnp.broadcast_to(SCALE * cos, (4, 128)), jnp.broadcast_to(SCALE * sin, (4, 128))], 0
    )
    to_smem = [
        pltpu.make_async_copy(ints, u0, s_a.at[2]),
        pltpu.make_async_copy(floats, r0s, s_a.at[3]),
    ]
    for copy in to_smem:
        copy.start()
    wide = lax.broadcasted_iota(jnp.int32, (1, SLOTS * WIN), 1)
    column = (wide - (wide // WIN) * WIN).astype(F32) * SCALE
    k8 = lax.broadcasted_iota(jnp.int32, (KS, 1), 0) * SIDE
    for j in range(JS):
        cos, sin, _, base = meet(expanded[0:1], wide // WIN, centre(an * 64 + j * SIDE), centre(k8))
        r0l[:, j * 768 : (j + 1) * 768] = base - column
    csl[...] = SCALE * cos
    ssh[...] = (SCALE * sin) * lax.broadcasted_iota(jnp.int32, (SIDE, 1), 0).astype(F32)

    def make_wt(k, _):
        for j in range(JS):
            base = r0l[pl.ds(k, 1), j * 768 : (j + 1) * 768]
            for g in range(SIDE):
                x = (base + csl[...] * float(g)) + ssh[...]
                value = jnp.maximum(0.0, SCALE - jnp.abs(x)).astype(BF16)
                wt[k, g * SIDE : (g + 1) * SIDE, j * 768 : (j + 1) * 768] = value
        return 0

    lax.fori_loop(0, KS, make_wt, 0)

    for copy in to_smem:
        copy.wait()
    columns = lax.broadcasted_iota(jnp.int32, (WIN, 1), 0).astype(F32) * SCALE
    cell = lax.broadcasted_iota(jnp.int32, (1, 256), 1)
    cell_g = (cell // SIDE).astype(F32)
    cell_h = (cell - (cell // SIDE) * SIDE).astype(F32)

    def make_w(t, _):
        b, k = t // KS, lax.rem(t, KS)
        for i in range(4):
            row = cell_g * r0s[KS * JS, b * 4 + i] + cell_h * r0s[KS * JS + 4, b * 4 + i]
            for j in range(JS):
                x = (row + r0s[k * JS + j, b * 4 + i]) - columns
                value = jnp.maximum(0.0, SCALE - jnp.abs(x)).astype(BF16)
                w[b, k, (i * JS + j) * WIN : (i * JS + j + 1) * WIN, :] = value
        return 0

    lax.fori_loop(0, BLK * KS, make_w, 0)

    local.wait()
    away.wait()

    def first(b, _):
        half, third = b // 3, lax.rem(b, 3)
        rows = mbuf[half, pl.ds(third * 4, 4)].reshape(192, 128)
        res[b] = fdot(sel0[...], rows)
        return 0

    lax.fori_loop(0, BLK, first, 0)

    def spread(src):
        def body(b, _):
            for i in range(4):
                rt = src(b)[i * BAND : (i + 1) * BAND, :].T.astype(BF16)
                sp = fdot(rt, zft[...]).astype(BF16).astype(F32)
                srep[pl.ds((b * 4 + i) * 16, 16)] = sp.reshape(16, 8, 128)
            return 0

        lax.fori_loop(0, BLK, body, 0)

    def back(lo, hi, put):
        def body(k, _):
            for j in range(JS):
                for a in range(SLOTS):
                    x = srep[pl.ds(a * 16 + u0[k * JS + j, a], WIN // 8)].reshape(WIN, 128)
                    spot = j * 768 + a * WIN
                    sk[spot : spot + WIN, :] = jnp.where(lane_group == j, x, 0.0).astype(BF16)
            put(pl.ds(pl.multiple_of(k * 256, 256), 256), fdot(wt[k], sk[...]))
            return 0

        lax.fori_loop(lo, hi, body, 0)

    def lines_copy(n, b):
        there = lax.rem(b + 3, BLK)
        return remote(lsend.at[n, b], lrecv.at[n, there], s_ls.at[n, b], s_lr.at[n, there], angle=1 - an)

    def up_copy(n, b):
        return remote(
            edge.at[n, b, pl.ds(0, 64)], halo.at[n, b, pl.ds(0, 64)], s_es.at[n, b, 0], s_er.at[n, b, 0],
            slab=lax.rem(sl + 1, 8),
        )

    def down_copy(n, b):
        return remote(
            edge.at[n, b, pl.ds(64, 64)], halo.at[n, b, pl.ds(64, 64)], s_es.at[n, b, 1], s_er.at[n, b, 1],
            slab=lax.rem(sl + 7, 8),
        )

    def project(vol, n):
        def multiply(b, buf):
            for k in range(KS):
                o = fdot(w[b, k], vol[k * 256 : (k + 1) * 256, :])
                for e in range(16):
                    at = (k * 16 + e) * 16 + PAD // 8
                    buf[at : at + WIN // 8] = o[e * WIN : (e + 1) * WIN].reshape(-1, 8, 128)

        def place(b, buf):
            packed = None
            for i in range(4):
                total = None
                for j in range(JS):
                    acc = None
                    for k in range(KS):
                        shift = u0[k * JS + j, b * 4 + i]
                        x = buf[pl.ds((k * 16 + i * JS + j) * 16 + PAD // 8 - shift, 16)]
                        acc = x if acc is None else acc + x
                    acc = acc.reshape(128, 128)
                    total = acc if total is None else jnp.where(lane_group == j, acc, total)
                total = total + pltpu.roll(total, 64, 1)
                total = total + pltpu.roll(total, 32, 1)
                packed = total if packed is None else jnp.where(lane_group == i, total, packed)
            lown[b] = packed
            lsend[n, b] = packed.astype(BF16)
            lines_copy(n, b).start()

        def body(t, _):
            b = lax.rem(2 * t + 3, BLK)
            multiply(lax.rem(2 * t + 4, BLK), rbuf2)
            place(b, rbuf)
            multiply(lax.rem(2 * t + 5, BLK), rbuf)
            place(lax.rem(2 * t + 4, BLK), rbuf2)
            return 0

        multiply(3, rbuf)
        lax.fori_loop(0, BLK // 2, body, 0)

    def partials(n):
        def body(t, _):
            b = t
            lines_copy(n, lax.rem(b + 3, BLK)).wait_recv()
            lines = (lown[b] + lrecv[n, b].astype(F32)).astype(BF16)
            pp = lax.dot_general(zf4[...], lines, (((1,), (1,)), ((), ())), preferred_element_type=F32).astype(BF16)
            part[b] = pp[:160].astype(F32)
            edge[n, b] = pp[160:]
            up_copy(n, b).start()
            down_copy(n, b).start()
            return 0

        lax.fori_loop(0, BLK, body, 0)

        def join(t, _):
            b = t
            up_copy(n, b).wait_recv()
            down_copy(n, b).wait_recv()
            img[n, b] = part[b] + fdot(sel4[...], halo[n, b])
            return 0

        lax.fori_loop(0, BLK, join, 0)

    def fold(x):
        return x.reshape(-1, 8, 128).sum(0)

    def stage_of(stage):
        return ((red1, "slab", sl, 8), (red2, "phase", ph, 8), (red3, "angle", an, 2))[stage]

    def stage_copies(n, stage, arriving):
        buf, axis, me, size = stage_of(stage)
        copies = []
        for d in range(1, size):
            to = lax.rem(me + d, size)
            slot = lax.rem(me + size - d, size) if arriving else me
            base = (0, 8, 16)[stage]
            place = buf.at[n, slot]
            copies.append(remote(place, place, s_rs.at[n, base + d], s_rr.at[n, base + slot], **{axis: to}))
        return copies

    def send_stage(n, stage, value):
        buf, _, me, _ = stage_of(stage)
        buf[n, me] = value
        for copy in stage_copies(n, stage, False):
            copy.start()

    def take_stage(n, stage):
        buf, _, _, size = stage_of(stage)
        for copy in stage_copies(n, stage, True):
            copy.wait_recv()
        total = buf[n, 0]
        for i in range(1, size):
            total = total + buf[n, i]
        return total

    spread(lambda b: res[b])

    def put_first(at, o):
        d0[at, :] = o
        d0b[at, :] = o.astype(BF16)

    back(0, KS, put_first)
    up_d = remote(d0b, nbr.at[0], s_vs.at[0], s_vr.at[0], phase=lax.rem(ph + 1, 8))
    down_d = remote(d0b, nbr.at[1], s_vs.at[1], s_vr.at[1], phase=lax.rem(ph + 7, 8))
    pair_d = remote(d0b, par_d, s_vs.at[2], s_vr.at[2], angle=1 - an)
    up_d.start()
    down_d.start()
    project(d0b, 0)
    partials(0)
    pair_d.start()

    spread(lambda b: img[0, b])
    up_d.wait_recv()
    down_d.wait_recv()
    zero = jnp.zeros((8, 128), F32)

    def first_sums(k, carry):
        gam, den = carry
        at = pl.ds(pl.multiple_of(k * 256, 256), 256)
        v = d0[at, :]
        p = 2.0 * v - nbr[0, at, :].astype(F32) - nbr[1, at, :].astype(F32)
        pd0[at, :] = p
        return gam + fold(v * v), den + fold(v * p)

    gam, den = lax.fori_loop(0, KS, first_sums, (zero, zero))

    def image_sums(b, den):
        im = img[0, b]
        return den + fold(own[...] * im * im)

    den = lax.fori_loop(0, 3, image_sums, den)

    def put_second(at, o):
        g1[at, :] = o

    send_stage(0, 0, jnp.concatenate([gam, den, zero], 0))
    back(0, 2, put_second)
    send_stage(0, 1, take_stage(0, 0))
    back(2, 5, put_second)
    send_stage(0, 2, take_stage(0, 1))
    back(5, KS, put_second)
    sums = take_stage(0, 2)
    gamma0 = jnp.sum(sums[0:8], axis=(0, 1), keepdims=True)
    den0 = jnp.sum(sums[8:16], axis=(0, 1), keepdims=True)
    alpha0 = gamma0 / den0

    def second_grad(k, carry):
        gam, cross = carry
        at = pl.ds(pl.multiple_of(k * 256, 256), 256)
        p = pd0[at, :]
        v = d0[at, :] - alpha0 * (g1[at, :] + p)
        g1[at, :] = v
        g1b[at, :] = v.astype(BF16)
        return gam + fold(v * v), cross + fold(v * p)

    gam, cross = lax.fori_loop(0, KS, second_grad, (zero, zero))
    half = ROWS // 2
    up_g = remote(g1b.at[pl.ds(0, half)], nbg.at[pl.ds(0, half)], s_vs.at[3], s_vr.at[3], phase=lax.rem(ph + 1, 8))
    down_g = remote(
        g1b.at[pl.ds(half, half)], nbg.at[pl.ds(half, half)], s_vs.at[4], s_vr.at[4], phase=lax.rem(ph + 7, 8)
    )
    pair_g = remote(g1b, par_g, s_vs.at[5], s_vr.at[5], angle=1 - an)
    up_g.start()
    down_g.start()
    project(g1b, 1)
    partials(1)
    pair_g.start()
    up_g.wait_recv()
    down_g.wait_recv()

    def second_sums(k, acc):
        at = pl.ds(pl.multiple_of(k * 256, 256), 256)
        return acc + fold(g1[at, :] * nbg[at, :].astype(F32))

    lag = lax.fori_loop(0, KS, second_sums, zero)

    def image_sums2(b, carry):
        den, cross = carry
        im = img[1, b]
        wi = own[...] * im
        return den + fold(wi * im), cross + fold(wi * img[0, b])

    den, cross = lax.fori_loop(0, 3, image_sums2, (2.0 * gam - 2.0 * lag, cross))
    send_stage(1, 0, jnp.concatenate([gam, den, cross], 0))

    def turn(src, dst, side):
        def body(g, _):
            cells = jnp.concatenate(
                [src[pl.ds(pl.multiple_of(k * 256 + g * SIDE, SIDE), SIDE), :].astype(F32) for k in range(KS)], 0
            ).T.astype(BF16)
            for j in range(JS):
                column = pl.multiple_of((side * 64 + j * SIDE + g) * 128, 128)
                dst[:, pl.ds(column, 128)] = cells[j * 32 : (j + 1) * 32]
            return 0

        lax.fori_loop(0, SIDE, body, 0)

    turn(d0b, out_d, an)
    send_stage(1, 1, take_stage(1, 0))
    pair_d.wait_recv()
    turn(par_d, out_d, 1 - an)
    send_stage(1, 2, take_stage(1, 1))
    turn(g1b, out_g, an)
    sums = take_stage(1, 2)
    gamma1 = jnp.sum(sums[0:8], axis=(0, 1), keepdims=True)
    den1 = jnp.sum(sums[8:16], axis=(0, 1), keepdims=True)
    cross1 = jnp.sum(sums[16:24], axis=(0, 1), keepdims=True)
    beta = gamma1 / gamma0
    alpha1 = gamma1 / (den1 + 2.0 * beta * cross1 + beta * beta * den0)
    c0 = alpha0 + alpha1 * beta
    out_c[...] = jnp.concatenate(
        [jnp.broadcast_to(c0, (8, 128)), jnp.broadcast_to(alpha1, (8, 128))], 0
    )

    def last(b, _):
        for i in range(4):
            at = slice(i * BAND, (i + 1) * BAND)
            out_r[0, b * 4 + i] = (
                jnp.where(an * OWN + b * 4 + i < count, res[b, at, :], 0.0) - c0 * img[0, b, at, :] - alpha1 * img[1, b, at, :]
            )
        return 0

    lax.fori_loop(0, 3, last, 0)
    pair_g.wait_recv()
    turn(par_g, out_g, 1 - an)

    for copy in (up_d, down_d, pair_d, up_g, down_g, pair_g):
        copy.wait_send()
    for n in range(2):

        def sent(b, _):
            lines_copy(n, b).wait_send()
            up_copy(n, b).wait_send()
            down_copy(n, b).wait_send()
            return 0

        lax.fori_loop(0, BLK, sent, 0)
        for stage in range(3):
            for copy in stage_copies(n, stage, False):
                copy.wait_send()


def combine(c_ref, d_ref, g_ref, out_ref):
    out_ref[0] = c_ref[0, 0] * d_ref[...].astype(F32) + c_ref[8, 0] * g_ref[...].astype(F32)


def per_device(measured, angles, counts, bands, zfoot):
    vmem, smem = pl.BlockSpec(memory_space=pltpu.VMEM), pl.BlockSpec(memory_space=pltpu.SMEM)
    volume16, volume32 = pltpu.VMEM((ROWS, 128), BF16), pltpu.VMEM((ROWS, 128), F32)
    placed = pltpu.VMEM((KS * 256 + PAD // 8, 8, 128), F32)
    out_d, out_g, out_c, out_r = pl.pallas_call(
        kernel,
        out_shape=(
            jax.ShapeDtypeStruct((CZ, GRID * GRID), BF16),
            jax.ShapeDtypeStruct((CZ, GRID * GRID), BF16),
            jax.ShapeDtypeStruct((16, 128), F32),
            jax.ShapeDtypeStruct((1, OWN, BAND, 128), F32),
        ),
        in_specs=[pl.BlockSpec(memory_space=pl.ANY), vmem, vmem, smem, smem],
        out_specs=(vmem,) * 4,
        scratch_shapes=[
            pltpu.VMEM((2, 8, 128), jnp.int32),
            pltpu.VMEM((KS * JS, 128), jnp.int32),
            pltpu.VMEM((KS * JS + 8, 128), F32),
            pltpu.SMEM((KS * JS, 128), jnp.int32),
            pltpu.SMEM((KS * JS + 8, 128), F32),
            pltpu.VMEM((KS, JS * SLOTS * WIN), F32),
            pltpu.VMEM((1, SLOTS * WIN), F32),
            pltpu.VMEM((SIDE, SLOTS * WIN), F32),
            pltpu.VMEM((BAND, 128), BF16),
            pltpu.VMEM((4 * BAND + 128, 128), BF16),
            pltpu.VMEM((4 * BAND, 128), BF16),
            pltpu.VMEM((4 * BAND, 192), BF16),
            pltpu.VMEM((4 * BAND, 128), F32),
            pltpu.VMEM((KS, 256, JS * SLOTS * WIN), BF16),
            pltpu.VMEM((BLK, KS, 16 * WIN, 256), BF16),
            placed, placed,
            pltpu.VMEM((JS * SLOTS * WIN, 128), BF16),
            pltpu.VMEM((SLOTS * 16, 8, 128), F32),
            pltpu.VMEM((2, OWN, 48, 128), BF16),
            pltpu.VMEM((BLK, 4 * BAND, 128), F32),
            volume32, volume32, volume32, volume16, volume16,
            pltpu.VMEM((2, ROWS, 128), BF16),
            volume16, volume16, volume16,
            pltpu.VMEM((BLK, 128, 128), F32),
            pltpu.VMEM((2, BLK, 128, 128), BF16),
            pltpu.VMEM((2, BLK, 128, 128), BF16),
            pltpu.VMEM((BLK, 4 * BAND, 128), F32),
            pltpu.VMEM((2, BLK, 4 * BAND, 128), F32),
            pltpu.VMEM((2, BLK, 128, 128), BF16),
            pltpu.VMEM((2, BLK, 128, 128), BF16),
            pltpu.VMEM((2, 8, 24, 128), F32),
            pltpu.VMEM((2, 8, 24, 128), F32),
            pltpu.VMEM((2, 2, 24, 128), F32),
            pltpu.SemaphoreType.DMA((4,)),
            pltpu.SemaphoreType.DMA((3,)),
            pltpu.SemaphoreType.DMA((6,)),
            pltpu.SemaphoreType.DMA((6,)),
            pltpu.SemaphoreType.DMA((2, BLK)),
            pltpu.SemaphoreType.DMA((2, BLK)),
            pltpu.SemaphoreType.DMA((2, BLK, 2)),
            pltpu.SemaphoreType.DMA((2, BLK, 2)),
            pltpu.SemaphoreType.DMA((2, 18)),
            pltpu.SemaphoreType.DMA((2, 18)),
        ],
        compiler_params=pltpu.CompilerParams(
            collective_id=0, has_side_effects=True, vmem_limit_bytes=60 * 1024 * 1024
        ),
    )(measured, angles, zfoot, counts, bands)
    chunk = 4096
    half = pl.BlockSpec((CZ, chunk), lambda i: (0, i))
    result = pl.pallas_call(
        combine,
        grid=(GRID * GRID // chunk,),
        out_shape=jax.ShapeDtypeStruct((1, CZ, GRID * GRID), F32),
        in_specs=[smem, half, half],
        out_specs=pl.BlockSpec((1, CZ, chunk), lambda i: (0, 0, i)),
    )(out_c, out_d, out_g)
    return result, out_r


def solution(mesh):
    placed = (P("phase", "angle", None, None), P("phase", "angle"), P(), P(), P("slab", None))
    return jax.shard_map(
        per_device,
        mesh=mesh,
        in_specs=placed,
        out_specs=(P("phase", "slab", None), P("phase", "angle", "slab", None)),
        check_vma=False,
    )
```

```python
import functools
import math

import jax
import jax.numpy as jnp
from jax import lax
from jax.experimental import pallas as pl
from jax.experimental.pallas import tpu as pltpu
from jax.sharding import PartitionSpec as P

GRID = 128
NVIEW = 640
CZ = 32
BAND = 40
SLOTS = 24
OWN = 12
SIDE = 16
WIN = 24
TILES = 5
PER = 5
POS = TILES * PER
LANES = TILES * 128
AWAY = (3, 4, 2, 0, 1)
LAST = GRID - WIN
KS = 8
JS = 4
SCALE = 1.0 / math.sqrt(GRID)
ROWS = KS * 256
F32 = jnp.float32
BF16 = jnp.bfloat16


def fdot(a, b):
    return jnp.dot(a, b, preferred_element_type=F32)


def remote(src, dst, send, recv, **where):
    return pltpu.make_async_remote_copy(
        src_ref=src,
        dst_ref=dst,
        send_sem=send,
        recv_sem=recv,
        device_id=where,
        device_id_type=pl.DeviceIdType.MESH,
    )


def kernel(
    meas, angles, zfoot, counts, bands,
    out_d, out_g, out_c, out_r,
    ang, ints, u0, r0l, gcs, ssh, zft, zf5, sel5, sel0, own,
    wt, vt, ob, ska, skb, srep, mbuf, res, d0, pd0, g1, d0b, g1b, nbr, nbg, par_d, par_g,
    lown, lsend, lrecv, part, img, edge, halo, red1, red2, red3,
    s_a, s_m, s_vs, s_vr, s_ls, s_lr, s_es, s_er, s_rs, s_rr,
):
    ph, sl, an = (lax.axis_index(n) for n in ("phase", "slab", "angle"))
    barrier = pltpu.get_barrier_semaphore()
    mesh_id = pl.DeviceIdType.MESH
    for d in range(1, 8):
        pl.semaphore_signal(barrier, 1, device_id={"slab": lax.rem(sl + d, 8)}, device_id_type=mesh_id)
        pl.semaphore_signal(barrier, 1, device_id={"phase": lax.rem(ph + d, 8)}, device_id_type=mesh_id)
    pl.semaphore_signal(barrier, 1, device_id={"angle": 1 - an}, device_id_type=mesh_id)
    pl.semaphore_wait(barrier, 15)

    ang[0] = jnp.pad(angles[...], ((0, 7), (0, 128 - OWN)))
    angles_out = remote(ang.at[0], ang.at[1], s_a.at[0], s_a.at[1], angle=1 - an)
    angles_out.start()
    band_rows = meas.at[0, :, pl.ds(pl.multiple_of(sl * CZ, CZ), 48), :]
    local = pltpu.make_async_copy(band_rows, mbuf.at[0:12], s_m.at[0])
    local.start()
    away = [
        remote(band_rows.at[0:10], mbuf.at[15:25], s_m.at[1], s_m.at[3], angle=1 - an),
        remote(band_rows.at[10:12], mbuf.at[13:15], s_m.at[2], s_m.at[4], angle=1 - an),
    ]
    for copy in away:
        copy.start()
    mbuf[12] = jnp.zeros((48, 128), BF16)

    lane = lax.broadcasted_iota(jnp.int32, (1, 128), 1)
    lane_group = lane // 32

    zt = zfoot[...].astype(F32).T
    zt = jnp.concatenate([zt] * 4, 1)
    zft[...] = zt.astype(BF16)
    slot_z = lax.broadcasted_iota(jnp.int32, (1, PER * CZ), 1) // CZ
    zt5 = jnp.concatenate([zt, zt[:, :CZ]], 1)
    groups = [jnp.where(slot_z == i, zt5, 0.0) for i in range(PER)]
    zf5[...] = jnp.concatenate(groups + [m[BAND - 16 :] for m in groups] + [m[:16] for m in groups], 0).astype(BF16)
    start = bands[sl]
    below, above = bands[jnp.maximum(sl - 1, 0)], bands[jnp.minimum(sl + 1, 7)]
    row = start + lax.broadcasted_iota(jnp.int32, (BAND, 1), 0)
    edge_lane = lax.broadcasted_iota(jnp.int32, (1, PER * 32), 1)
    lower = edge_lane < PER * 16
    sixteenth = edge_lane - (edge_lane // 16) * 16
    other_row = jnp.where(lower, below + BAND - 16, above) + sixteenth
    there = jnp.where(lower, sl, 7 - sl) > 0
    slot_e = edge_lane // 16 - jnp.where(lower, 0, PER)
    sel5[...] = jnp.concatenate(
        [((row == other_row) & (there & (slot_e == i))).astype(F32) for i in range(PER)], 0
    ).astype(BF16)
    wide = lax.broadcasted_iota(jnp.int32, (1, PER * 48), 1)
    sel0[...] = jnp.concatenate(
        [(row - sl * CZ == wide - 48 * i).astype(F32) for i in range(PER)], 0
    ).astype(BF16)
    mine = ((row >= below + BAND) | (sl == 0)).astype(F32)
    own[...] = jnp.concatenate([jnp.broadcast_to(mine, (BAND, 128))] * PER, 0)

    angles_out.wait()
    theirs = jnp.where(lane < 15, pltpu.roll(ang[1], 3, 1), pltpu.roll(ang[1], 15, 1))
    both = jnp.where(lane < OWN, ang[0], theirs).astype(F32)
    slot_of = lax.broadcasted_iota(jnp.int32, (128, LANES), 0)
    wide = lax.broadcasted_iota(jnp.int32, (1, LANES), 1)
    window = (wide - (wide // 128) * 128) // WIN
    lane_slot = jnp.where(window < PER, (wide // 128) * PER + window, 127)
    one_hot = (slot_of == lane_slot).astype(F32)
    expanded = jnp.dot(both, one_hot, precision=lax.Precision.HIGHEST, preferred_element_type=F32)
    count = counts[ph]

    def meet(angle, slot, left, low):
        theta = angle * F32(math.pi / NVIEW)
        cos, sin = jnp.cos(theta), jnp.sin(theta)
        other = jnp.where(slot < 15, slot - 3, slot - 15)
        ident = jnp.where(slot < OWN, an * OWN + slot, (1 - an) * OWN + other)
        alive = (ident < count) & (slot != OWN) & (slot < POS)
        corner = left * cos + low * sin
        least = corner + (SIDE - 1) * (jnp.minimum(cos, 0.0) + jnp.minimum(sin, 0.0))
        first = jnp.clip(jnp.floor(least + (GRID / 2 - 1.5 - 1e-3)) + 1.0, 0.0, float(LAST))
        base = SCALE * (corner - first + (GRID / 2 - 0.5))
        return cos, sin, first, jnp.where(alive, base, 1e3)

    def centre(i):
        return i.astype(F32) + (0.5 - GRID / 2)

    block = lax.broadcasted_iota(jnp.int32, (KS * JS, 1), 0)
    along = block // JS
    cos, sin, first, _ = meet(
        both[0:1], lane, centre(an * 64 + (block - along * JS) * SIDE), centre(along * SIDE)
    )
    first = jnp.clip(first.astype(jnp.int32), 0, LAST)
    turned = first - (lane - (lane // PER) * PER) * WIN
    ints[0 : KS * JS, :] = first
    ints[KS * JS :, :] = jnp.clip(jnp.where(turned < 0, turned + 128, turned), 0, 127)
    to_smem = pltpu.make_async_copy(ints, u0, s_a.at[2])
    to_smem.start()
    column = (wide - (wide // 128) * 128 - window * WIN).astype(F32) * SCALE
    k8 = lax.broadcasted_iota(jnp.int32, (KS, 1), 0) * SIDE
    for j in range(JS):
        cos, sin, _, base = meet(expanded[0:1], lane_slot, centre(an * 64 + j * SIDE), centre(k8))
        r0l[:, j * LANES : (j + 1) * LANES] = base - column
    side = lax.broadcasted_iota(jnp.int32, (SIDE, 1), 0).astype(F32)
    gcs[...] = (SCALE * cos) * side
    ssh[...] = (SCALE * sin) * side

    def make_wt(k, _):
        for j in range(JS):
            start = r0l[pl.ds(k, 1), j * LANES : (j + 1) * LANES] + ssh[...]
            for g in range(SIDE):
                x = start + gcs[g : g + 1, :]
                value = jnp.maximum((SCALE - jnp.abs(x)).astype(BF16), 0)
                wt[k, g * SIDE : (g + 1) * SIDE, j * LANES : (j + 1) * LANES] = value
        return 0

    lax.fori_loop(0, KS, make_wt, 0)

    local.wait()
    for copy in away:
        copy.wait()
    for t in range(TILES):
        rows = mbuf[t * PER : (t + 1) * PER].reshape(PER * 48, 128)
        res[t] = fdot(sel0[...], rows)
    to_smem.wait()

    def spread(src):
        def body(t, _):
            for i in range(PER):
                rt = src(t)[i * BAND : (i + 1) * BAND, :].T.astype(BF16)
                sp = fdot(rt, zft[...]).astype(BF16).astype(F32)
                srep[pl.ds(pl.multiple_of((t * PER + i) * 128, 128), 128), :] = sp
            return 0

        lax.fori_loop(0, TILES, body, 0)

    def gather(k, sk):
        for j in range(JS):
            for t in range(TILES):
                x = jnp.concatenate(
                    [srep[pl.ds((t * PER + i) * 128 + u0[k * JS + j, t * PER + i], WIN), :] for i in range(PER)], 0
                )
                x = jnp.concatenate([jnp.where(lane_group == j, x, 0.0), jnp.zeros((128 - PER * WIN, 128), F32)], 0)
                sk[j * LANES + t * 128 : j * LANES + (t + 1) * 128, :] = x.astype(BF16)

    def back(lo, hi, put):
        def multiply(k, sk):
            put(pl.ds(pl.multiple_of(k * 256, 256), 256), fdot(wt[k], sk[...]))

        def body(q, _):
            k = 2 * q
            gather(k + 1, skb)
            multiply(k, ska)
            gather(jnp.minimum(k + 2, KS - 1), ska)
            multiply(k + 1, skb)
            return 0

        lax.fori_loop(lo // 2, hi // 2, body, 0)

    def lines_copy(n, t):
        there = AWAY[t]
        return remote(lsend.at[n, t], lrecv.at[n, there], s_ls.at[n, t], s_lr.at[n, there], angle=1 - an)

    def up_copy(n, t):
        return remote(
            edge.at[n, t, pl.ds(0, 80)], halo.at[n, t, pl.ds(0, 80)], s_es.at[n, t, 0], s_er.at[n, t, 0],
            slab=lax.rem(sl + 1, 8),
        )

    def down_copy(n, t):
        return remote(
            edge.at[n, t, pl.ds(80, 80)], halo.at[n, t, pl.ds(80, 80)], s_es.at[n, t, 1], s_er.at[n, t, 1],
            slab=lax.rem(sl + 7, 8),
        )

    def project(vol, n):
        def multiply(q, _):
            for d in range(2):
                k = 2 * q + d
                for h in range(2):
                    at = pl.multiple_of(k * 256 + h * 128, 128)
                    vt[k, :, h * 128 : (h + 1) * 128] = vol[pl.ds(at, 128), :].T
                for j in range(JS):
                    ob[k * JS + j] = fdot(
                        vt[k, j * CZ : (j + 1) * CZ, :], wt[k, :, j * LANES : (j + 1) * LANES]
                    )
            return 0

        lax.fori_loop(0, KS // 2, multiply, 0)
        for t in range(TILES):

            def place(q, sums):
                sums = list(sums)
                for e in range(16):
                    b = q * 16 + e
                    x = ob[b, :, t * 128 : (t + 1) * 128]
                    for i in range(PER):
                        window = jnp.where((lane >= WIN * i) & (lane < WIN * (i + 1)), x, 0.0)
                        sums[i] = sums[i] + pltpu.roll(window, u0[KS * JS + b, t * PER + i], 1)
                return tuple(sums)

            sums = lax.fori_loop(0, KS * JS // 16, place, tuple(jnp.zeros((CZ, 128), F32) for _ in range(PER)))
            lown[t] = jnp.concatenate(sums, 0)
            if t == 2:
                sums = (sums[3], sums[4], sums[2], sums[0], sums[1])
            lsend[n, t] = jnp.concatenate(sums, 0).astype(BF16)
            lines_copy(n, t).start()

    def partials(n):
        for t in AWAY:
            lines_copy(n, AWAY[t]).wait_recv()
            lines = (lown[t] + lrecv[n, t].astype(F32)).astype(BF16)
            pp = fdot(zf5[...], lines).astype(BF16)
            part[t] = pp[: PER * BAND].astype(F32)
            edge[n, t] = pp[PER * BAND :]
            up_copy(n, t).start()
            down_copy(n, t).start()
        for t in AWAY:
            up_copy(n, t).wait_recv()
            down_copy(n, t).wait_recv()
            img[n, t] = part[t] + fdot(sel5[...], halo[n, t])

    def fold(x):
        return x.reshape(-1, 8, 128).sum(0)

    def stage_of(stage):
        return ((red1, "slab", sl, 8), (red2, "phase", ph, 8), (red3, "angle", an, 2))[stage]

    def stage_copies(n, stage, arriving):
        buf, axis, me, size = stage_of(stage)
        copies = []
        for d in range(1, size):
            to = lax.rem(me + d, size)
            slot = lax.rem(me + size - d, size) if arriving else me
            base = (0, 8, 16)[stage]
            place = buf.at[n, slot]
            copies.append(remote(place, place, s_rs.at[n, base + d], s_rr.at[n, base + slot], **{axis: to}))
        return copies

    def send_stage(n, stage, value):
        buf, _, me, _ = stage_of(stage)
        buf[n, me] = value
        for copy in stage_copies(n, stage, False):
            copy.start()

    def take_stage(n, stage):
        buf, _, _, size = stage_of(stage)
        for copy in stage_copies(n, stage, True):
            copy.wait_recv()
        total = buf[n, 0]
        for i in range(1, size):
            total = total + buf[n, i]
        return total

    spread(lambda b: res[b])

    def put_first(at, o):
        d0[at, :] = o
        d0b[at, :] = o.astype(BF16)

    gather(0, ska)
    back(0, KS, put_first)
    up_d = remote(d0b, nbr.at[0], s_vs.at[0], s_vr.at[0], phase=lax.rem(ph + 1, 8))
    down_d = remote(d0b, nbr.at[1], s_vs.at[1], s_vr.at[1], phase=lax.rem(ph + 7, 8))
    pair_d = remote(d0b, par_d, s_vs.at[2], s_vr.at[2], angle=1 - an)
    up_d.start()
    down_d.start()
    project(d0b, 0)
    partials(0)
    pair_d.start()

    spread(lambda b: img[0, b])
    up_d.wait_recv()
    down_d.wait_recv()
    zero = jnp.zeros((8, 128), F32)

    def first_sums(k, carry):
        gam, den = carry
        at = pl.ds(pl.multiple_of(k * 256, 256), 256)
        v = d0[at, :]
        p = 2.0 * v - nbr[0, at, :].astype(F32) - nbr[1, at, :].astype(F32)
        pd0[at, :] = p
        return gam + fold(v * v), den + fold(v * p)

    gam, den = lax.fori_loop(0, KS, first_sums, (zero, zero))

    for t, rows in ((0, PER * BAND), (1, PER * BAND), (2, 2 * BAND)):
        im = img[0, t, :rows]
        den = den + fold(own[:rows] * im * im)

    def put_second(at, o):
        g1[at, :] = o

    send_stage(0, 0, jnp.concatenate([gam, den, zero], 0))
    gather(0, ska)
    back(0, 2, put_second)
    send_stage(0, 1, take_stage(0, 0))
    back(2, 4, put_second)
    send_stage(0, 2, take_stage(0, 1))
    back(4, KS, put_second)
    sums = take_stage(0, 2)
    gamma0 = jnp.sum(sums[0:8], axis=(0, 1), keepdims=True)
    den0 = jnp.sum(sums[8:16], axis=(0, 1), keepdims=True)
    alpha0 = gamma0 / den0

    def second_grad(k, carry):
        gam, cross = carry
        at = pl.ds(pl.multiple_of(k * 256, 256), 256)
        p = pd0[at, :]
        v = d0[at, :] - alpha0 * (g1[at, :] + p)
        g1[at, :] = v
        g1b[at, :] = v.astype(BF16)
        return gam + fold(v * v), cross + fold(v * p)

    gam, cross = lax.fori_loop(0, KS, second_grad, (zero, zero))
    half = ROWS // 2
    up_g = remote(g1b.at[pl.ds(0, half)], nbg.at[pl.ds(0, half)], s_vs.at[3], s_vr.at[3], phase=lax.rem(ph + 1, 8))
    down_g = remote(
        g1b.at[pl.ds(half, half)], nbg.at[pl.ds(half, half)], s_vs.at[4], s_vr.at[4], phase=lax.rem(ph + 7, 8)
    )
    pair_g = remote(g1b, par_g, s_vs.at[5], s_vr.at[5], angle=1 - an)
    up_g.start()
    down_g.start()
    project(g1b, 1)
    partials(1)
    pair_g.start()
    up_g.wait_recv()
    down_g.wait_recv()

    def second_sums(k, acc):
        at = pl.ds(pl.multiple_of(k * 256, 256), 256)
        return acc + fold(g1[at, :] * nbg[at, :].astype(F32))

    lag = lax.fori_loop(0, KS, second_sums, zero)

    den = 2.0 * gam - 2.0 * lag
    for t, rows in ((0, PER * BAND), (1, PER * BAND), (2, 2 * BAND)):
        im = img[1, t, :rows]
        wi = own[:rows] * im
        den, cross = den + fold(wi * im), cross + fold(wi * img[0, t, :rows])
    send_stage(1, 0, jnp.concatenate([gam, den, cross], 0))

    def turn(src, dst, side):
        def body(g, _):
            cells = jnp.concatenate(
                [src[pl.ds(pl.multiple_of(k * 256 + g * SIDE, SIDE), SIDE), :].astype(F32) for k in range(KS)], 0
            ).T.astype(BF16)
            for j in range(JS):
                column = pl.multiple_of((side * 64 + j * SIDE + g) * 128, 128)
                dst[:, pl.ds(column, 128)] = cells[j * 32 : (j + 1) * 32]
            return 0

        lax.fori_loop(0, SIDE, body, 0)

    turn(d0b, out_d, an)
    send_stage(1, 1, take_stage(1, 0))
    pair_d.wait_recv()
    turn(par_d, out_d, 1 - an)
    send_stage(1, 2, take_stage(1, 1))
    turn(g1b, out_g, an)
    sums = take_stage(1, 2)
    gamma1 = jnp.sum(sums[0:8], axis=(0, 1), keepdims=True)
    den1 = jnp.sum(sums[8:16], axis=(0, 1), keepdims=True)
    cross1 = jnp.sum(sums[16:24], axis=(0, 1), keepdims=True)
    beta = gamma1 / gamma0
    alpha1 = gamma1 / (den1 + 2.0 * beta * cross1 + beta * beta * den0)
    c0 = alpha0 + alpha1 * beta
    out_c[...] = jnp.concatenate(
        [jnp.broadcast_to(c0, (8, 128)), jnp.broadcast_to(alpha1, (8, 128))], 0
    )

    for a in range(OWN):
        t, at = a // PER, slice((a % PER) * BAND, (a % PER + 1) * BAND)
        out_r[0, a] = (
            jnp.where(an * OWN + a < count, res[t, at, :], 0.0) - c0 * img[0, t, at, :] - alpha1 * img[1, t, at, :]
        )
    pair_g.wait_recv()
    turn(par_g, out_g, 1 - an)

    for copy in (up_d, down_d, pair_d, up_g, down_g, pair_g):
        copy.wait_send()
    for n in range(2):

        for t in range(TILES):
            lines_copy(n, t).wait_send()
            up_copy(n, t).wait_send()
            down_copy(n, t).wait_send()
        for stage in range(3):
            for copy in stage_copies(n, stage, False):
                copy.wait_send()


def combine(c_ref, d_ref, g_ref, out_ref):
    out_ref[0] = c_ref[0, 0] * d_ref[...].astype(F32) + c_ref[8, 0] * g_ref[...].astype(F32)


def per_device(measured, angles, counts, bands, zfoot):
    vmem, smem = pl.BlockSpec(memory_space=pltpu.VMEM), pl.BlockSpec(memory_space=pltpu.SMEM)
    volume16, volume32 = pltpu.VMEM((ROWS, 128), BF16), pltpu.VMEM((ROWS, 128), F32)
    out_d, out_g, out_c, out_r = pl.pallas_call(
        kernel,
        out_shape=(
            jax.ShapeDtypeStruct((CZ, GRID * GRID), BF16),
            jax.ShapeDtypeStruct((CZ, GRID * GRID), BF16),
            jax.ShapeDtypeStruct((16, 128), F32),
            jax.ShapeDtypeStruct((1, OWN, BAND, 128), F32),
        ),
        in_specs=[pl.BlockSpec(memory_space=pl.ANY), vmem, vmem, smem, smem],
        out_specs=(vmem,) * 4,
        scratch_shapes=[
            pltpu.VMEM((2, 8, 128), jnp.int32),
            pltpu.VMEM((2 * KS * JS, 128), jnp.int32),
            pltpu.SMEM((2 * KS * JS, 128), jnp.int32),
            pltpu.VMEM((KS, JS * LANES), F32),
            pltpu.VMEM((SIDE, LANES), F32),
            pltpu.VMEM((SIDE, LANES), F32),
            pltpu.VMEM((BAND, 128), BF16),
            pltpu.VMEM((PER * (BAND + 32), PER * CZ), BF16),
            pltpu.VMEM((PER * BAND, PER * 32), BF16),
            pltpu.VMEM((PER * BAND, PER * 48), BF16),
            pltpu.VMEM((PER * BAND, 128), F32),
            pltpu.VMEM((KS, 256, JS * LANES), BF16),
            pltpu.VMEM((KS, 128, 256), BF16),
            pltpu.VMEM((KS * JS, CZ, LANES), F32),
            pltpu.VMEM((JS * LANES, 128), BF16),
            pltpu.VMEM((JS * LANES, 128), BF16),
            pltpu.VMEM((POS * 128, 128), F32),
            pltpu.VMEM((POS, 48, 128), BF16),
            pltpu.VMEM((TILES, PER * BAND, 128), F32),
            volume32, volume32, volume32, volume16, volume16,
            pltpu.VMEM((2, ROWS, 128), BF16),
            volume16, volume16, volume16,
            pltpu.VMEM((TILES, PER * CZ, 128), F32),
            pltpu.VMEM((2, TILES, PER * CZ, 128), BF16),
            pltpu.VMEM((2, TILES, PER * CZ, 128), BF16),
            pltpu.VMEM((TILES, PER * BAND, 128), F32),
            pltpu.VMEM((2, TILES, PER * BAND, 128), F32),
            pltpu.VMEM((2, TILES, PER * 32, 128), BF16),
            pltpu.VMEM((2, TILES, PER * 32, 128), BF16),
            pltpu.VMEM((2, 8, 24, 128), F32),
            pltpu.VMEM((2, 8, 24, 128), F32),
            pltpu.VMEM((2, 2, 24, 128), F32),
            pltpu.SemaphoreType.DMA((3,)),
            pltpu.SemaphoreType.DMA((5,)),
            pltpu.SemaphoreType.DMA((6,)),
            pltpu.SemaphoreType.DMA((6,)),
            pltpu.SemaphoreType.DMA((2, TILES)),
            pltpu.SemaphoreType.DMA((2, TILES)),
            pltpu.SemaphoreType.DMA((2, TILES, 2)),
            pltpu.SemaphoreType.DMA((2, TILES, 2)),
            pltpu.SemaphoreType.DMA((2, 18)),
            pltpu.SemaphoreType.DMA((2, 18)),
        ],
        compiler_params=pltpu.CompilerParams(
            collective_id=0, has_side_effects=True, vmem_limit_bytes=60 * 1024 * 1024
        ),
    )(measured, angles, zfoot, counts, bands)
    chunk = 4096
    half = pl.BlockSpec((CZ, chunk), lambda i: (0, i))
    result = pl.pallas_call(
        combine,
        grid=(GRID * GRID // chunk,),
        out_shape=jax.ShapeDtypeStruct((1, CZ, GRID * GRID), F32),
        in_specs=[smem, half, half],
        out_specs=pl.BlockSpec((1, CZ, chunk), lambda i: (0, 0, i)),
    )(out_c, out_d, out_g)
    return result, out_r


def solution(mesh):
    placed = (P("phase", "angle", None, None), P("phase", "angle"), P(), P(), P("slab", None))
    return jax.shard_map(
        per_device,
        mesh=mesh,
        in_specs=placed,
        out_specs=(P("phase", "slab", None), P("phase", "angle", "slab", None)),
        check_vma=False,
    )
```

```python
import functools
import math

import jax
import jax.numpy as jnp
from jax import lax
from jax.experimental import pallas as pl
from jax.experimental.pallas import tpu as pltpu
from jax.sharding import PartitionSpec as P

GRID = 128
NVIEW = 640
CZ = 32
BAND = 40
SLOTS = 24
OWN = 12
SIDE = 16
WIN = 24
TILES = 5
PER = 5
POS = TILES * PER
LANES = TILES * 128
AWAY = (3, 4, 2, 0, 1)
LAST = GRID - WIN
KS = 8
JS = 4
SCALE = 1.0 / math.sqrt(GRID)
ROWS = KS * 256
F32 = jnp.float32
BF16 = jnp.bfloat16


def fdot(a, b):
    return jnp.dot(a, b, preferred_element_type=F32)


def remote(src, dst, send, recv, **where):
    return pltpu.make_async_remote_copy(
        src_ref=src,
        dst_ref=dst,
        send_sem=send,
        recv_sem=recv,
        device_id=where,
        device_id_type=pl.DeviceIdType.MESH,
    )


def kernel(
    meas, angles, zfoot, counts, bands,
    out_d, out_g, out_c, out_r,
    ang, ints, u0, r0l, gcs, ssh, zft, zf5, sel5, sel0, own,
    wt, vt, ob, ska, skb, srep, mbuf, res, d0, pd0, g1, d0b, g1b, nbr, nbg, par_d, par_g,
    lown, lsend, lrecv, part, img, edge, halo, red1, red2,
    s_a, s_m, s_ds, s_dr, s_vs, s_vr, s_ls, s_lr, s_es, s_er, s_rs, s_rr,
):
    ph, sl, an = (lax.axis_index(n) for n in ("phase", "slab", "angle"))
    barrier = pltpu.get_barrier_semaphore()
    place = ph * 2 + an

    def at_place(i):
        return {"phase": i // 2, "angle": lax.rem(i, 2)}

    for d in range(1, 8):
        pl.semaphore_signal(
            barrier, 1, device_id={"slab": lax.rem(sl + d, 8)}, device_id_type=pl.DeviceIdType.MESH
        )
    for d in range(1, 16):
        pl.semaphore_signal(
            barrier, 1, device_id=at_place(lax.rem(place + d, 16)), device_id_type=pl.DeviceIdType.MESH
        )
    band_rows = meas.at[0, :, pl.ds(pl.multiple_of(sl * CZ, CZ), 48), :]
    local = pltpu.make_async_copy(band_rows, mbuf.at[0:12], s_m.at[0])
    local.start()
    mbuf[12] = jnp.zeros((48, 128), BF16)
    ang[0] = jnp.pad(angles[...], ((0, 7), (0, 128 - OWN)))

    lane = lax.broadcasted_iota(jnp.int32, (1, 128), 1)
    lane_group = lane // 32

    zt = zfoot[...].astype(F32).T
    zt = jnp.concatenate([zt] * 4, 1)
    zft[...] = zt.astype(BF16)
    slot_z = lax.broadcasted_iota(jnp.int32, (1, PER * CZ), 1) // CZ
    zt5 = jnp.concatenate([zt, zt[:, :CZ]], 1)
    groups = [jnp.where(slot_z == i, zt5, 0.0) for i in range(PER)]
    zf5[...] = jnp.concatenate(groups + [m[BAND - 16 :] for m in groups] + [m[:16] for m in groups], 0).astype(BF16)
    start = bands[sl]
    below, above = bands[jnp.maximum(sl - 1, 0)], bands[jnp.minimum(sl + 1, 7)]
    row = start + lax.broadcasted_iota(jnp.int32, (BAND, 1), 0)
    edge_lane = lax.broadcasted_iota(jnp.int32, (1, PER * 32), 1)
    lower = edge_lane < PER * 16
    sixteenth = edge_lane - (edge_lane // 16) * 16
    other_row = jnp.where(lower, below + BAND - 16, above) + sixteenth
    there = jnp.where(lower, sl, 7 - sl) > 0
    slot_e = edge_lane // 16 - jnp.where(lower, 0, PER)
    sel5[...] = jnp.concatenate(
        [((row == other_row) & (there & (slot_e == i))).astype(F32) for i in range(PER)], 0
    ).astype(BF16)
    wide = lax.broadcasted_iota(jnp.int32, (1, PER * 48), 1)
    sel0[...] = jnp.concatenate(
        [(row - sl * CZ == wide - 48 * i).astype(F32) for i in range(PER)], 0
    ).astype(BF16)
    mine = ((row >= below + BAND) | (sl == 0)).astype(F32)
    own[...] = jnp.concatenate([jnp.broadcast_to(mine, (BAND, 128))] * PER, 0)

    pl.semaphore_wait(barrier, 22)
    angles_out = remote(ang.at[0], ang.at[1], s_a.at[0], s_a.at[1], angle=1 - an)
    angles_out.start()
    away = [
        remote(band_rows.at[0:10], mbuf.at[15:25], s_m.at[1], s_m.at[3], angle=1 - an),
        remote(band_rows.at[10:12], mbuf.at[13:15], s_m.at[2], s_m.at[4], angle=1 - an),
    ]
    for copy in away:
        copy.start()

    count = counts[ph]

    def meet(angle, slot, left, low):
        theta = angle * F32(math.pi / NVIEW)
        cos, sin = jnp.cos(theta), jnp.sin(theta)
        other = jnp.where(slot < 15, slot - 3, slot - 15)
        ident = jnp.where(slot < OWN, an * OWN + slot, (1 - an) * OWN + other)
        alive = (ident < count) & (slot != OWN) & (slot < POS)
        corner = left * cos + low * sin
        least = corner + (SIDE - 1) * (jnp.minimum(cos, 0.0) + jnp.minimum(sin, 0.0))
        first = jnp.clip(jnp.floor(least + (GRID / 2 - 1.5 - 1e-3)) + 1.0, 0.0, float(LAST))
        base = SCALE * (corner - first + (GRID / 2 - 0.5))
        return cos, sin, first, jnp.where(alive, base, 1e3)

    def centre(i):
        return i.astype(F32) + (0.5 - GRID / 2)

    k8 = lax.broadcasted_iota(jnp.int32, (KS, 1), 0) * SIDE
    side = lax.broadcasted_iota(jnp.int32, (SIDE, 1), 0).astype(F32)

    def weigh(positions, lo, hi):
        lanes = hi - lo
        slot_of = lax.broadcasted_iota(jnp.int32, (128, lanes), 0)
        wide = lax.broadcasted_iota(jnp.int32, (1, lanes), 1) + lo
        window = (wide - (wide // 128) * 128) // WIN
        lane_slot = jnp.where(window < PER, (wide // 128) * PER + window, 127)
        expanded = jnp.dot(
            positions, (slot_of == lane_slot).astype(F32),
            precision=lax.Precision.HIGHEST, preferred_element_type=F32,
        )
        column = (wide - (wide // 128) * 128 - window * WIN).astype(F32) * SCALE
        for j in range(JS):
            cos, sin, _, base = meet(expanded[0:1], lane_slot, centre(an * 64 + j * SIDE), centre(k8))
            r0l[:, j * LANES + lo : j * LANES + hi] = base - column
        gcs[:, lo:hi] = (SCALE * cos) * side
        ssh[:, lo:hi] = (SCALE * sin) * side

        def make_wt(k, _):
            for j in range(JS):
                start = r0l[pl.ds(k, 1), j * LANES : (j + 1) * LANES][:, lo:hi] + ssh[:, lo:hi]
                for g in range(SIDE):
                    x = start + gcs[g : g + 1, lo:hi]
                    value = jnp.maximum((SCALE - jnp.abs(x)).astype(BF16), 0)
                    wt[k, g * SIDE : (g + 1) * SIDE, j * LANES + lo : j * LANES + hi] = value
            return 0

        lax.fori_loop(0, KS, make_wt, 0)

    weigh(ang[0].astype(F32), 0, 256)
    angles_out.wait()
    theirs = jnp.where(lane < 15, pltpu.roll(ang[1], 3, 1), pltpu.roll(ang[1], 15, 1))
    both = jnp.where(lane < OWN, ang[0], theirs).astype(F32)
    block = lax.broadcasted_iota(jnp.int32, (KS * JS, 1), 0)
    along = block // JS
    _, _, first, _ = meet(
        both[0:1], lane, centre(an * 64 + (block - along * JS) * SIDE), centre(along * SIDE)
    )
    first = jnp.clip(first.astype(jnp.int32), 0, LAST)
    turned = first - (lane - (lane // PER) * PER) * WIN
    ints[0 : KS * JS, :] = first
    ints[KS * JS :, :] = jnp.clip(jnp.where(turned < 0, turned + 128, turned), 0, 127)
    to_smem = pltpu.make_async_copy(ints, u0, s_a.at[2])
    to_smem.start()
    weigh(both, 256, LANES)

    local.wait()
    for copy in away:
        copy.wait()
    for t in range(TILES):
        rows = mbuf[t * PER : (t + 1) * PER].reshape(PER * 48, 128)
        res[t] = fdot(sel0[...], rows)

    def spread(t, rows):
        for i in range(PER):
            rt = rows[i * BAND : (i + 1) * BAND, :].T.astype(BF16)
            at = (t * PER + i) * 128
            srep[at : at + 128, :] = fdot(rt, zft[...]).astype(BF16).astype(F32)

    def gather(k, sk):
        for j in range(JS):
            for t in range(TILES):
                x = jnp.concatenate(
                    [srep[pl.ds((t * PER + i) * 128 + u0[k * JS + j, t * PER + i], WIN), :] for i in range(PER)], 0
                )
                x = jnp.concatenate([jnp.where(lane_group == j, x, 0.0), jnp.zeros((128 - PER * WIN, 128), F32)], 0)
                sk[j * LANES + t * 128 : j * LANES + (t + 1) * 128, :] = x.astype(BF16)

    def back(lo, hi, put, then=None):
        def multiply(k, sk):
            put(pl.ds(pl.multiple_of(k * 256, 256), 256), fdot(wt[k], sk[...]))

        def body(q, _):
            k = 2 * q
            gather(k + 1, skb)
            multiply(k, ska)
            gather(jnp.minimum(k + 2, KS - 1), ska)
            multiply(k + 1, skb)
            if then is not None:
                then(q)
            return 0

        lax.fori_loop(lo // 2, hi // 2, body, 0)

    def lines_copy(n, t):
        there = AWAY[t]
        return remote(lsend.at[n, t], lrecv.at[n, there], s_ls.at[n, t], s_lr.at[n, there], angle=1 - an)

    def up_copy(n, t):
        return remote(
            edge.at[n, t, pl.ds(0, 80)], halo.at[n, t, pl.ds(0, 80)], s_es.at[n, t, 0], s_er.at[n, t, 0],
            slab=lax.rem(sl + 1, 8),
        )

    def down_copy(n, t):
        return remote(
            edge.at[n, t, pl.ds(80, 80)], halo.at[n, t, pl.ds(80, 80)], s_es.at[n, t, 1], s_er.at[n, t, 1],
            slab=lax.rem(sl + 7, 8),
        )

    def project(vol, n, sent):
        def multiply(q, _):
            for d in range(2):
                k = 2 * q + d
                for h in range(2):
                    at = pl.multiple_of(k * 256 + h * 128, 128)
                    vt[k, :, h * 128 : (h + 1) * 128] = vol[pl.ds(at, 128), :].T
                for j in range(JS):
                    ob[k * JS + j] = fdot(
                        vt[k, j * CZ : (j + 1) * CZ, :], wt[k, :, j * LANES : (j + 1) * LANES]
                    )
            return 0

        lax.fori_loop(0, KS // 2, multiply, 0)
        for t in AWAY:

            def place(q, sums):
                sums = list(sums)
                for e in range(16):
                    b = q * 16 + e
                    x = ob[b, :, t * 128 : (t + 1) * 128]
                    for i in range(PER):
                        window = jnp.where((lane >= WIN * i) & (lane < WIN * (i + 1)), x, 0.0)
                        sums[i] = sums[i] + pltpu.roll(window, u0[KS * JS + b, t * PER + i], 1)
                return tuple(sums)

            sums = lax.fori_loop(0, KS * JS // 16, place, tuple(jnp.zeros((CZ, 128), F32) for _ in range(PER)))
            lown[t] = jnp.concatenate(sums, 0)
            if n == 0 or t >= 2:
                if t == 2:
                    sums = (sums[3], sums[4], sums[2], sums[0], sums[1])
                lsend[n, t] = jnp.concatenate(sums, 0).astype(BF16)
                lines_copy(n, t).start()
            if t == 2:
                sent()
            if t == 0:
                partial(n, 0)
            if t == 1:
                partial(n, 1)
                partial(n, 2)

    def partial(n, t):
        lines_copy(n, AWAY[t]).wait_recv()
        lines = (lown[t] + lrecv[n, t].astype(F32)).astype(BF16)
        pp = fdot(zf5[...], lines).astype(BF16)
        part[t] = pp[: PER * BAND].astype(F32)
        edge[n, t] = pp[PER * BAND :]
        up_copy(n, t).start()
        down_copy(n, t).start()

    def join(n, t):
        up_copy(n, t).wait_recv()
        down_copy(n, t).wait_recv()
        img[n, t] = part[t] + fdot(sel5[...], halo[n, t])

    def fold(x):
        return x.reshape(-1, 8, 128).sum(0)

    def stage_copies(n, stage, arriving):
        buf, me, size = ((red1, sl, 8), (red2, place, 16))[stage]
        copies = []
        for d in range(1, size):
            to = lax.rem(me + d, size)
            slot = lax.rem(me + size - d, size) if arriving else me
            spot = buf.at[n, slot]
            where = at_place(to) if stage else {"slab": to}
            copies.append(remote(spot, spot, s_rs.at[n, stage * 8 + d], s_rr.at[n, stage * 8 + slot], **where))
        return copies

    def send_stage(n, stage, value):
        buf, me = ((red1, sl), (red2, place))[stage]
        buf[n, me] = value
        for copy in stage_copies(n, stage, False):
            copy.start()

    def take_stage(n, stage):
        buf, size = ((red1, 8), (red2, 16))[stage]
        for copy in stage_copies(n, stage, True):
            copy.wait_recv()
        values = [buf[n, i] for i in range(size)]
        while len(values) > 1:
            values = [values[i] + values[i + 1] for i in range(0, len(values), 2)]
        return values[0]

    def rows_of(*values):
        rows = [v.sum(0, keepdims=True) for v in values]
        return jnp.concatenate(rows + [jnp.zeros((8 - len(rows), 128), F32)], 0)

    def turn(src, dst, side):
        def body(g, _):
            cells = jnp.concatenate(
                [src[pl.ds(pl.multiple_of(k * 256 + g * SIDE, SIDE), SIDE), :] for k in range(KS)], 0
            ).T
            for j in range(JS):
                column = pl.multiple_of((side * 64 + j * SIDE + g) * 128, 128)
                dst[:, pl.ds(column, 128)] = cells[j * 32 : (j + 1) * 32]
            return 0

        lax.fori_loop(0, SIDE, body, 0)

    for t in range(TILES):
        spread(t, res[t])
    to_smem.wait()

    def put_first(at, o):
        d0[at, :] = o
        d0b[at, :] = o.astype(BF16)

    def to_phases(q):
        at = pl.ds(pl.multiple_of(q * 512, 512), 512)
        return [
            remote(d0b.at[at], nbr.at[0, at], s_ds.at[0, q], s_dr.at[0, q], phase=lax.rem(ph + 1, 8)),
            remote(d0b.at[at], nbr.at[1, at], s_ds.at[1, q], s_dr.at[1, q], phase=lax.rem(ph + 7, 8)),
        ]

    def go(q):
        for copy in to_phases(q):
            copy.start()

    gather(0, ska)
    back(0, KS, put_first, go)
    pair_d = remote(d0b, par_d, s_vs.at[0], s_vr.at[0], angle=1 - an)
    project(d0b, 0, lambda: None)
    turn(d0b, out_d, an)
    partial(0, 3)
    partial(0, 4)
    pair_d.start()

    zero = jnp.zeros((8, 128), F32)

    def first_sums(q, carry):
        gam, den = carry
        for copy in to_phases(q):
            copy.wait_recv()
        at = pl.ds(pl.multiple_of(q * 512, 512), 512)
        v = d0[at, :]
        p = 2.0 * v - nbr[0, at, :].astype(F32) - nbr[1, at, :].astype(F32)
        pd0[at, :] = p
        return gam + fold(v * v), den + fold(v * p)

    gam, den = lax.fori_loop(0, KS // 2, first_sums, (zero, zero))
    own_rows = ((0, PER * BAND), (1, PER * BAND), (2, 2 * BAND))
    for t, rows in own_rows:
        join(0, t)
        im = img[0, t, :rows]
        den = den + fold(own[:rows] * im * im)
    send_stage(0, 0, rows_of(gam, den))
    for t in range(3):
        spread(t, img[0, t])
    for t in (3, 4):
        join(0, t)
        spread(t, img[0, t])

    def put_second(at, o):
        g1[at, :] = o

    gather(0, ska)
    back(0, 4, put_second)
    send_stage(0, 1, take_stage(0, 0))
    back(4, KS, put_second)
    sums = take_stage(0, 1)
    gamma0 = jnp.sum(sums[0:1], axis=(0, 1), keepdims=True)
    den0 = jnp.sum(sums[1:2], axis=(0, 1), keepdims=True)
    alpha0 = gamma0 / den0

    def second_grad(k, carry):
        gam, cross = carry
        at = pl.ds(pl.multiple_of(k * 256, 256), 256)
        p = pd0[at, :]
        v = d0[at, :] - alpha0 * (g1[at, :] + p)
        g1[at, :] = v
        g1b[at, :] = v.astype(BF16)
        return gam + fold(v * v), cross + fold(v * p)

    gam, cross = lax.fori_loop(0, KS, second_grad, (zero, zero))
    half = ROWS // 2
    up_g = remote(g1b.at[pl.ds(0, half)], nbg.at[pl.ds(0, half)], s_vs.at[1], s_vr.at[1], phase=lax.rem(ph + 1, 8))
    down_g = remote(
        g1b.at[pl.ds(half, half)], nbg.at[pl.ds(half, half)], s_vs.at[2], s_vr.at[2], phase=lax.rem(ph + 7, 8)
    )
    pair_g = remote(g1b, par_g, s_vs.at[3], s_vr.at[3], angle=1 - an)
    up_g.start()
    down_g.start()
    project(g1b, 1, pair_g.start)
    pair_d.wait_recv()
    turn(par_d, out_d, 1 - an)
    up_g.wait_recv()
    down_g.wait_recv()

    def second_sums(k, acc):
        at = pl.ds(pl.multiple_of(k * 256, 256), 256)
        return acc + fold(g1[at, :] * nbg[at, :].astype(F32))

    lag = lax.fori_loop(0, KS, second_sums, zero)
    den = 2.0 * gam - 2.0 * lag
    for t, rows in own_rows:
        join(1, t)
        im = img[1, t, :rows]
        wi = own[:rows] * im
        den, cross = den + fold(wi * im), cross + fold(wi * img[0, t, :rows])
    send_stage(1, 0, rows_of(gam, den, cross))
    turn(g1b, out_g, an)
    send_stage(1, 1, take_stage(1, 0))
    pair_g.wait_recv()
    turn(par_g, out_g, 1 - an)
    sums = take_stage(1, 1)
    gamma1 = jnp.sum(sums[0:1], axis=(0, 1), keepdims=True)
    den1 = jnp.sum(sums[1:2], axis=(0, 1), keepdims=True)
    cross1 = jnp.sum(sums[2:3], axis=(0, 1), keepdims=True)
    beta = gamma1 / gamma0
    alpha1 = gamma1 / (den1 + 2.0 * beta * cross1 + beta * beta * den0)
    c0 = alpha0 + alpha1 * beta
    out_c[...] = jnp.concatenate(
        [jnp.broadcast_to(c0, (8, 128)), jnp.broadcast_to(alpha1, (8, 128))], 0
    )

    for a in range(OWN):
        t, at = a // PER, slice((a % PER) * BAND, (a % PER + 1) * BAND)
        out_r[0, a] = (
            jnp.where(an * OWN + a < count, res[t, at, :], 0.0) - c0 * img[0, t, at, :] - alpha1 * img[1, t, at, :]
        )

    for copy in (pair_d, up_g, down_g, pair_g):
        copy.wait_send()

    def gone(q, _):
        for copy in to_phases(q):
            copy.wait_send()
        return 0

    lax.fori_loop(0, KS // 2, gone, 0)
    for n in range(2):
        for t in range(TILES):
            if n == 0 or t >= 2:
                lines_copy(n, t).wait_send()
            if n == 0 or t <= 2:
                up_copy(n, t).wait_send()
                down_copy(n, t).wait_send()
        for stage in range(2):
            for copy in stage_copies(n, stage, False):
                copy.wait_send()


def combine(c_ref, d_ref, g_ref, r_ref, out_ref, res_ref):
    out_ref[0] = c_ref[0, 0] * d_ref[...].astype(F32) + c_ref[8, 0] * g_ref[...].astype(F32)
    res_ref[...] = r_ref[...]


def per_device(measured, angles, counts, bands, zfoot):
    vmem, smem = pl.BlockSpec(memory_space=pltpu.VMEM), pl.BlockSpec(memory_space=pltpu.SMEM)
    volume16, volume32 = pltpu.VMEM((ROWS, 128), BF16), pltpu.VMEM((ROWS, 128), F32)
    out_d, out_g, out_c, out_r = pl.pallas_call(
        kernel,
        out_shape=(
            jax.ShapeDtypeStruct((CZ, GRID * GRID), BF16),
            jax.ShapeDtypeStruct((CZ, GRID * GRID), BF16),
            jax.ShapeDtypeStruct((16, 128), F32),
            jax.ShapeDtypeStruct((1, OWN, BAND, 128), F32),
        ),
        in_specs=[pl.BlockSpec(memory_space=pl.ANY), vmem, vmem, smem, smem],
        out_specs=(vmem,) * 4,
        scratch_shapes=[
            pltpu.VMEM((2, 8, 128), jnp.int32),
            pltpu.VMEM((2 * KS * JS, 128), jnp.int32),
            pltpu.SMEM((2 * KS * JS, 128), jnp.int32),
            pltpu.VMEM((KS, JS * LANES), F32),
            pltpu.VMEM((SIDE, LANES), F32),
            pltpu.VMEM((SIDE, LANES), F32),
            pltpu.VMEM((BAND, 128), BF16),
            pltpu.VMEM((PER * (BAND + 32), PER * CZ), BF16),
            pltpu.VMEM((PER * BAND, PER * 32), BF16),
            pltpu.VMEM((PER * BAND, PER * 48), BF16),
            pltpu.VMEM((PER * BAND, 128), F32),
            pltpu.VMEM((KS, 256, JS * LANES), BF16),
            pltpu.VMEM((KS, 128, 256), BF16),
            pltpu.VMEM((KS * JS, CZ, LANES), F32),
            pltpu.VMEM((JS * LANES, 128), BF16),
            pltpu.VMEM((JS * LANES, 128), BF16),
            pltpu.VMEM((POS * 128, 128), F32),
            pltpu.VMEM((POS, 48, 128), BF16),
            pltpu.VMEM((TILES, PER * BAND, 128), F32),
            volume32, volume32, volume32, volume16, volume16,
            pltpu.VMEM((2, ROWS, 128), BF16),
            volume16, volume16, volume16,
            pltpu.VMEM((TILES, PER * CZ, 128), F32),
            pltpu.VMEM((2, TILES, PER * CZ, 128), BF16),
            pltpu.VMEM((2, TILES, PER * CZ, 128), BF16),
            pltpu.VMEM((TILES, PER * BAND, 128), F32),
            pltpu.VMEM((2, TILES, PER * BAND, 128), F32),
            pltpu.VMEM((2, TILES, PER * 32, 128), BF16),
            pltpu.VMEM((2, TILES, PER * 32, 128), BF16),
            pltpu.VMEM((2, 8, 8, 128), F32),
            pltpu.VMEM((2, 16, 8, 128), F32),
            pltpu.SemaphoreType.DMA((3,)),
            pltpu.SemaphoreType.DMA((5,)),
            pltpu.SemaphoreType.DMA((2, KS // 2)),
            pltpu.SemaphoreType.DMA((2, KS // 2)),
            pltpu.SemaphoreType.DMA((4,)),
            pltpu.SemaphoreType.DMA((4,)),
            pltpu.SemaphoreType.DMA((2, TILES)),
            pltpu.SemaphoreType.DMA((2, TILES)),
            pltpu.SemaphoreType.DMA((2, TILES, 2)),
            pltpu.SemaphoreType.DMA((2, TILES, 2)),
            pltpu.SemaphoreType.DMA((2, 24)),
            pltpu.SemaphoreType.DMA((2, 24)),
        ],
        compiler_params=pltpu.CompilerParams(
            collective_id=0, has_side_effects=True, vmem_limit_bytes=60 * 1024 * 1024
        ),
    )(measured, angles, zfoot, counts, bands)
    chunk = 8192
    half = pl.BlockSpec((CZ, chunk), lambda i: (0, i))
    rows = pl.BlockSpec((1, OWN, BAND, 128), lambda i: (0, 0, 0, 0))
    return pl.pallas_call(
        combine,
        grid=(GRID * GRID // chunk,),
        out_shape=(
            jax.ShapeDtypeStruct((1, CZ, GRID * GRID), F32),
            jax.ShapeDtypeStruct((1, OWN, BAND, 128), F32),
        ),
        in_specs=[smem, half, half, rows],
        out_specs=(pl.BlockSpec((1, CZ, chunk), lambda i: (0, 0, i)), rows),
    )(out_c, out_d, out_g, out_r)


def solution(mesh):
    placed = (P("phase", "angle", None, None), P("phase", "angle"), P(), P(), P("slab", None))
    return jax.shard_map(
        per_device,
        mesh=mesh,
        in_specs=placed,
        out_specs=(P("phase", "slab", None), P("phase", "angle", "slab", None)),
        check_vma=False,
    )
```

```python
import functools
import math

import jax
import jax.numpy as jnp
from jax import lax
from jax.experimental import pallas as pl
from jax.experimental.pallas import tpu as pltpu
from jax.sharding import PartitionSpec as P

GRID = 128
NVIEW = 640
CZ = 32
BAND = 40
SLOTS = 24
OWN = 12
SIDE = 16
WIN = 24
TILES = 5
PER = 5
POS = TILES * PER
LANES = TILES * 128
AWAY = (3, 4, 2, 0, 1)
LAST = GRID - WIN
KS = 8
JS = 4
SCALE = 1.0 / math.sqrt(GRID)
ROWS = KS * 256
F32 = jnp.float32
BF16 = jnp.bfloat16


def fdot(a, b):
    return jnp.dot(a, b, preferred_element_type=F32)


def remote(src, dst, send, recv, **where):
    return pltpu.make_async_remote_copy(
        src_ref=src,
        dst_ref=dst,
        send_sem=send,
        recv_sem=recv,
        device_id=where,
        device_id_type=pl.DeviceIdType.MESH,
    )


def kernel(
    meas, angles, zfoot, counts, bands,
    out_d, out_g, out_c, out_r,
    ang, ints, u0, r0l, gcs, ssh, zft, zf5, sel5, sel0, own,
    wt, vt, ob01, ob2, ob34, ska, skb, srep, mbuf, res, d0, pd0, g1, d0b, g1b, nbr, nbg, par_d, par_g,
    lown, lsend, lrecv, part, img, edge, halo, red1, red2,
    s_a, s_m, s_ds, s_dr, s_vs, s_vr, s_ls, s_lr, s_es, s_er, s_rs, s_rr,
):
    ph, sl, an = (lax.axis_index(n) for n in ("phase", "slab", "angle"))
    barrier = pltpu.get_barrier_semaphore()
    place = ph * 2 + an

    def at_place(i):
        return {"phase": i // 2, "angle": lax.rem(i, 2)}

    for d in range(1, 8):
        pl.semaphore_signal(
            barrier, 1, device_id={"slab": lax.rem(sl + d, 8)}, device_id_type=pl.DeviceIdType.MESH
        )
    for d in range(1, 16):
        pl.semaphore_signal(
            barrier, 1, device_id=at_place(lax.rem(place + d, 16)), device_id_type=pl.DeviceIdType.MESH
        )
    band_rows = meas.at[0, :, pl.ds(pl.multiple_of(sl * CZ, CZ), 48), :]
    local = pltpu.make_async_copy(band_rows, mbuf.at[0:12], s_m.at[0])
    local.start()
    mbuf[12] = jnp.zeros((48, 128), BF16)
    ang[0] = jnp.pad(angles[...], ((0, 7), (0, 128 - OWN)))

    lane = lax.broadcasted_iota(jnp.int32, (1, 128), 1)
    lane_group = lane // 32

    zt = zfoot[...].astype(F32).T
    zt = jnp.concatenate([zt] * 4, 1)
    zft[...] = zt.astype(BF16)
    slot_z = lax.broadcasted_iota(jnp.int32, (1, PER * CZ), 1) // CZ
    zt5 = jnp.concatenate([zt, zt[:, :CZ]], 1)
    groups = [jnp.where(slot_z == i, zt5, 0.0) for i in range(PER)]
    zf5[...] = jnp.concatenate(groups + [m[BAND - 16 :] for m in groups] + [m[:16] for m in groups], 0).astype(BF16)
    start = bands[sl]
    below, above = bands[jnp.maximum(sl - 1, 0)], bands[jnp.minimum(sl + 1, 7)]
    row = start + lax.broadcasted_iota(jnp.int32, (BAND, 1), 0)
    edge_lane = lax.broadcasted_iota(jnp.int32, (1, PER * 32), 1)
    lower = edge_lane < PER * 16
    sixteenth = edge_lane - (edge_lane // 16) * 16
    other_row = jnp.where(lower, below + BAND - 16, above) + sixteenth
    there = jnp.where(lower, sl, 7 - sl) > 0
    slot_e = edge_lane // 16 - jnp.where(lower, 0, PER)
    sel5[...] = jnp.concatenate(
        [((row == other_row) & (there & (slot_e == i))).astype(F32) for i in range(PER)], 0
    ).astype(BF16)
    wide = lax.broadcasted_iota(jnp.int32, (1, PER * 48), 1)
    sel0[...] = jnp.concatenate(
        [(row - sl * CZ == wide - 48 * i).astype(F32) for i in range(PER)], 0
    ).astype(BF16)
    mine = ((row >= below + BAND) | (sl == 0)).astype(F32)
    own[...] = jnp.concatenate([jnp.broadcast_to(mine, (BAND, 128))] * PER, 0)

    pl.semaphore_wait(barrier, 22)
    angles_out = remote(ang.at[0], ang.at[1], s_a.at[0], s_a.at[1], angle=1 - an)
    angles_out.start()
    away = [
        remote(band_rows.at[0:10], mbuf.at[15:25], s_m.at[1], s_m.at[3], angle=1 - an),
        remote(band_rows.at[10:12], mbuf.at[13:15], s_m.at[2], s_m.at[4], angle=1 - an),
    ]
    for copy in away:
        copy.start()

    count = counts[ph]

    def meet(angle, slot, left, low):
        theta = angle * F32(math.pi / NVIEW)
        cos, sin = jnp.cos(theta), jnp.sin(theta)
        other = jnp.where(slot < 15, slot - 3, slot - 15)
        ident = jnp.where(slot < OWN, an * OWN + slot, (1 - an) * OWN + other)
        alive = (ident < count) & (slot != OWN) & (slot < POS)
        corner = left * cos + low * sin
        least = corner + (SIDE - 1) * (jnp.minimum(cos, 0.0) + jnp.minimum(sin, 0.0))
        first = jnp.clip(jnp.floor(least + (GRID / 2 - 1.5 - 1e-3)) + 1.0, 0.0, float(LAST))
        base = SCALE * (corner - first + (GRID / 2 - 0.5))
        return cos, sin, first, jnp.where(alive, base, 1e3)

    def centre(i):
        return i.astype(F32) + (0.5 - GRID / 2)

    k8 = lax.broadcasted_iota(jnp.int32, (KS, 1), 0) * SIDE
    side = lax.broadcasted_iota(jnp.int32, (SIDE, 1), 0).astype(F32)

    def weigh(positions, lo, hi):
        lanes = hi - lo
        slot_of = lax.broadcasted_iota(jnp.int32, (128, lanes), 0)
        wide = lax.broadcasted_iota(jnp.int32, (1, lanes), 1) + lo
        window = (wide - (wide // 128) * 128) // WIN
        lane_slot = jnp.where(window < PER, (wide // 128) * PER + window, 127)
        expanded = jnp.dot(
            positions, (slot_of == lane_slot).astype(F32),
            precision=lax.Precision.HIGHEST, preferred_element_type=F32,
        )
        column = (wide - (wide // 128) * 128 - window * WIN).astype(F32) * SCALE
        for j in range(JS):
            cos, sin, _, base = meet(expanded[0:1], lane_slot, centre(an * 64 + j * SIDE), centre(k8))
            r0l[:, j * LANES + lo : j * LANES + hi] = base - column
        gcs[:, lo:hi] = (SCALE * cos) * side
        ssh[:, lo:hi] = (SCALE * sin) * side

        def make_wt(k, _):
            for j in range(JS):
                start = r0l[pl.ds(k, 1), j * LANES : (j + 1) * LANES][:, lo:hi] + ssh[:, lo:hi]
                for g in range(SIDE):
                    x = start + gcs[g : g + 1, lo:hi]
                    value = jnp.maximum((SCALE - jnp.abs(x)).astype(BF16), 0)
                    wt[k, g * SIDE : (g + 1) * SIDE, j * LANES + lo : j * LANES + hi] = value
            return 0

        lax.fori_loop(0, KS, make_wt, 0)

    weigh(ang[0].astype(F32), 0, 256)
    angles_out.wait()
    theirs = jnp.where(lane < 15, pltpu.roll(ang[1], 3, 1), pltpu.roll(ang[1], 15, 1))
    both = jnp.where(lane < OWN, ang[0], theirs).astype(F32)
    block = lax.broadcasted_iota(jnp.int32, (KS * JS, 1), 0)
    along = block // JS
    _, _, first, _ = meet(
        both[0:1], lane, centre(an * 64 + (block - along * JS) * SIDE), centre(along * SIDE)
    )
    first = jnp.clip(first.astype(jnp.int32), 0, LAST)
    turned = first - (lane - (lane // PER) * PER) * WIN
    ints[0 : KS * JS, :] = first
    ints[KS * JS :, :] = jnp.clip(jnp.where(turned < 0, turned + 128, turned), 0, 127)
    to_smem = pltpu.make_async_copy(ints, u0, s_a.at[2])
    to_smem.start()
    weigh(both, 256, LANES)

    local.wait()
    for copy in away:
        copy.wait()
    for t in range(TILES):
        rows = mbuf[t * PER : (t + 1) * PER].reshape(PER * 48, 128)
        res[t] = fdot(sel0[...], rows)

    def spread(t, rows):
        for i in range(PER):
            rt = rows[i * BAND : (i + 1) * BAND, :].T.astype(BF16)
            at = (t * PER + i) * 128
            srep[at : at + 128, :] = fdot(rt, zft[...]).astype(BF16).astype(F32)

    def gather(k, sk):
        for j in range(JS):
            for t in range(TILES):
                x = jnp.concatenate(
                    [srep[pl.ds((t * PER + i) * 128 + u0[k * JS + j, t * PER + i], WIN), :] for i in range(PER)], 0
                )
                x = jnp.concatenate([jnp.where(lane_group == j, x, 0.0), jnp.zeros((128 - PER * WIN, 128), F32)], 0)
                sk[j * LANES + t * 128 : j * LANES + (t + 1) * 128, :] = x.astype(BF16)

    def back(lo, hi, put, then=None):
        def multiply(k, sk):
            put(pl.ds(pl.multiple_of(k * 256, 256), 256), fdot(wt[k], sk[...]))

        def body(q, _):
            k = 2 * q
            gather(k + 1, skb)
            multiply(k, ska)
            gather(jnp.minimum(k + 2, KS - 1), ska)
            multiply(k + 1, skb)
            if then is not None:
                then(q)
            return 0

        lax.fori_loop(lo // 2, hi // 2, body, 0)

    def lines_copy(n, t):
        there = AWAY[t]
        return remote(lsend.at[n, t], lrecv.at[n, there], s_ls.at[n, t], s_lr.at[n, there], angle=1 - an)

    def up_copy(n, t):
        return remote(
            edge.at[n, t, pl.ds(0, 80)], halo.at[n, t, pl.ds(0, 80)], s_es.at[n, t, 0], s_er.at[n, t, 0],
            slab=lax.rem(sl + 1, 8),
        )

    def down_copy(n, t):
        return remote(
            edge.at[n, t, pl.ds(80, 80)], halo.at[n, t, pl.ds(80, 80)], s_es.at[n, t, 1], s_er.at[n, t, 1],
            slab=lax.rem(sl + 7, 8),
        )

    def project(vol, n, sent):
        def multiply(k, buf, lo, hi):
            for j in range(JS):
                buf[k * JS + j] = fdot(vt[k, j * CZ : (j + 1) * CZ, :], wt[k, :, j * LANES + lo : j * LANES + hi])

        def begin(q, _):
            for k in (2 * q, 2 * q + 1):
                for h in range(2):
                    at = pl.multiple_of(k * 256 + h * 128, 128)
                    vt[k, :, h * 128 : (h + 1) * 128] = vol[pl.ds(at, 128), :].T
                multiply(k, ob34, 384, 640)
            return 0

        lax.fori_loop(0, KS // 2, begin, 0)
        for t in AWAY:
            buf, shift = ((ob01, 0), (ob01, 128), (ob2, 0), (ob34, 0), (ob34, 128))[t]

            def place(q, sums):
                sums = list(sums)
                for e in range(16):
                    b = q * 16 + e
                    x = buf[b, :, shift : shift + 128]
                    for i in range(PER):
                        window = jnp.where((lane >= WIN * i) & (lane < WIN * (i + 1)), x, 0.0)
                        sums[i] = sums[i] + pltpu.roll(window, u0[KS * JS + b, t * PER + i], 1)
                    if t == 3 and e % 4 == 0:
                        multiply(q * 4 + e // 4, ob01, 0, 256)
                    if t == 4 and e % 4 == 0:
                        multiply(q * 4 + e // 4, ob2, 256, 384)
                return tuple(sums)

            sums = lax.fori_loop(0, KS * JS // 16, place, tuple(jnp.zeros((CZ, 128), F32) for _ in range(PER)))
            lown[t] = jnp.concatenate(sums, 0)
            if n == 0 or t >= 2:
                if t == 2:
                    sums = (sums[3], sums[4], sums[2], sums[0], sums[1])
                lsend[n, t] = jnp.concatenate(sums, 0).astype(BF16)
                lines_copy(n, t).start()
            if t == 2:
                sent()
            if t == 0:
                partial(n, 0)
            if t == 1:
                partial(n, 1)
                partial(n, 2)

    def partial(n, t):
        lines_copy(n, AWAY[t]).wait_recv()
        lines = (lown[t] + lrecv[n, t].astype(F32)).astype(BF16)
        pp = fdot(zf5[...], lines).astype(BF16)
        part[t] = pp[: PER * BAND].astype(F32)
        edge[n, t] = pp[PER * BAND :]
        up_copy(n, t).start()
        down_copy(n, t).start()

    def join(n, t):
        up_copy(n, t).wait_recv()
        down_copy(n, t).wait_recv()
        img[n, t] = part[t] + fdot(sel5[...], halo[n, t])

    def fold(x):
        return x.reshape(-1, 8, 128).sum(0)

    def stage_copies(n, stage, arriving):
        buf, me, size = ((red1, sl, 8), (red2, place, 16))[stage]
        copies = []
        for d in range(1, size):
            to = lax.rem(me + d, size)
            slot = lax.rem(me + size - d, size) if arriving else me
            spot = buf.at[n, slot]
            where = at_place(to) if stage else {"slab": to}
            copies.append(remote(spot, spot, s_rs.at[n, stage * 8 + d], s_rr.at[n, stage * 8 + slot], **where))
        return copies

    def send_stage(n, stage, value):
        buf, me = ((red1, sl), (red2, place))[stage]
        buf[n, me] = value
        for copy in stage_copies(n, stage, False):
            copy.start()

    def take_stage(n, stage):
        buf, size = ((red1, 8), (red2, 16))[stage]
        for copy in stage_copies(n, stage, True):
            copy.wait_recv()
        values = [buf[n, i] for i in range(size)]
        while len(values) > 1:
            values = [values[i] + values[i + 1] for i in range(0, len(values), 2)]
        return values[0]

    def rows_of(*values):
        rows = [v.sum(0, keepdims=True) for v in values]
        return jnp.concatenate(rows + [jnp.zeros((8 - len(rows), 128), F32)], 0)

    def turn(src, dst, side):
        def body(g, _):
            cells = jnp.concatenate(
                [src[pl.ds(pl.multiple_of(k * 256 + g * SIDE, SIDE), SIDE), :] for k in range(KS)], 0
            ).T
            for j in range(JS):
                column = pl.multiple_of((side * 64 + j * SIDE + g) * 128, 128)
                dst[:, pl.ds(column, 128)] = cells[j * 32 : (j + 1) * 32]
            return 0

        lax.fori_loop(0, SIDE, body, 0)

    for t in range(TILES):
        spread(t, res[t])
    to_smem.wait()

    def put_first(at, o):
        d0[at, :] = o
        d0b[at, :] = o.astype(BF16)

    def to_phases(q):
        at = pl.ds(pl.multiple_of(q * 512, 512), 512)
        return [
            remote(d0b.at[at], nbr.at[0, at], s_ds.at[0, q], s_dr.at[0, q], phase=lax.rem(ph + 1, 8)),
            remote(d0b.at[at], nbr.at[1, at], s_ds.at[1, q], s_dr.at[1, q], phase=lax.rem(ph + 7, 8)),
        ]

    def go(q):
        for copy in to_phases(q):
            copy.start()

    gather(0, ska)
    back(0, KS, put_first, go)
    pair_d = remote(d0b, par_d, s_vs.at[0], s_vr.at[0], angle=1 - an)
    project(d0b, 0, lambda: None)
    pair_d.start()
    turn(d0b, out_d, an)
    partial(0, 3)
    partial(0, 4)

    zero = jnp.zeros((8, 128), F32)

    def first_sums(q, carry):
        gam, den = carry
        for copy in to_phases(q):
            copy.wait_recv()
        at = pl.ds(pl.multiple_of(q * 512, 512), 512)
        v = d0[at, :]
        p = 2.0 * v - nbr[0, at, :].astype(F32) - nbr[1, at, :].astype(F32)
        pd0[at, :] = p
        return gam + fold(v * v), den + fold(v * p)

    gam, den = lax.fori_loop(0, KS // 2, first_sums, (zero, zero))
    own_rows = ((0, PER * BAND), (1, PER * BAND), (2, 2 * BAND))
    for t, rows in own_rows:
        join(0, t)
        im = img[0, t, :rows]
        den = den + fold(own[:rows] * im * im)
    send_stage(0, 0, rows_of(gam, den))
    for t in range(3):
        spread(t, img[0, t])
    for t in (3, 4):
        join(0, t)
        spread(t, img[0, t])

    def put_second(at, o):
        g1[at, :] = o

    gather(0, ska)
    back(0, 4, put_second)
    send_stage(0, 1, take_stage(0, 0))
    back(4, KS, put_second)
    sums = take_stage(0, 1)
    gamma0 = jnp.sum(sums[0:1], axis=(0, 1), keepdims=True)
    den0 = jnp.sum(sums[1:2], axis=(0, 1), keepdims=True)
    alpha0 = gamma0 / den0

    def second_grad(k, carry):
        gam, cross = carry
        at = pl.ds(pl.multiple_of(k * 256, 256), 256)
        p = pd0[at, :]
        v = d0[at, :] - alpha0 * (g1[at, :] + p)
        g1[at, :] = v
        g1b[at, :] = v.astype(BF16)
        return gam + fold(v * v), cross + fold(v * p)

    gam, cross = lax.fori_loop(0, KS, second_grad, (zero, zero))
    half = ROWS // 2
    up_g = remote(g1b.at[pl.ds(0, half)], nbg.at[pl.ds(0, half)], s_vs.at[1], s_vr.at[1], phase=lax.rem(ph + 1, 8))
    down_g = remote(
        g1b.at[pl.ds(half, half)], nbg.at[pl.ds(half, half)], s_vs.at[2], s_vr.at[2], phase=lax.rem(ph + 7, 8)
    )
    pair_g = remote(g1b, par_g, s_vs.at[3], s_vr.at[3], angle=1 - an)
    up_g.start()
    down_g.start()
    project(g1b, 1, pair_g.start)
    pair_d.wait_recv()
    turn(par_d, out_d, 1 - an)
    up_g.wait_recv()
    down_g.wait_recv()

    def second_sums(k, acc):
        at = pl.ds(pl.multiple_of(k * 256, 256), 256)
        return acc + fold(g1[at, :] * nbg[at, :].astype(F32))

    lag = lax.fori_loop(0, KS, second_sums, zero)
    den = 2.0 * gam - 2.0 * lag
    for t, rows in own_rows:
        join(1, t)
        im = img[1, t, :rows]
        wi = own[:rows] * im
        den, cross = den + fold(wi * im), cross + fold(wi * img[0, t, :rows])
    send_stage(1, 0, rows_of(gam, den, cross))
    turn(g1b, out_g, an)
    send_stage(1, 1, take_stage(1, 0))
    pair_g.wait_recv()
    turn(par_g, out_g, 1 - an)
    sums = take_stage(1, 1)
    gamma1 = jnp.sum(sums[0:1], axis=(0, 1), keepdims=True)
    den1 = jnp.sum(sums[1:2], axis=(0, 1), keepdims=True)
    cross1 = jnp.sum(sums[2:3], axis=(0, 1), keepdims=True)
    beta = gamma1 / gamma0
    alpha1 = gamma1 / (den1 + 2.0 * beta * cross1 + beta * beta * den0)
    c0 = alpha0 + alpha1 * beta
    out_c[...] = jnp.concatenate(
        [jnp.broadcast_to(c0, (8, 128)), jnp.broadcast_to(alpha1, (8, 128))], 0
    )

    for a in range(OWN):
        t, at = a // PER, slice((a % PER) * BAND, (a % PER + 1) * BAND)
        out_r[0, a] = (
            jnp.where(an * OWN + a < count, res[t, at, :], 0.0) - c0 * img[0, t, at, :] - alpha1 * img[1, t, at, :]
        )

    for copy in (pair_d, up_g, down_g, pair_g):
        copy.wait_send()

    def gone(q, _):
        for copy in to_phases(q):
            copy.wait_send()
        return 0

    lax.fori_loop(0, KS // 2, gone, 0)
    for n in range(2):
        for t in range(TILES):
            if n == 0 or t >= 2:
                lines_copy(n, t).wait_send()
            if n == 0 or t <= 2:
                up_copy(n, t).wait_send()
                down_copy(n, t).wait_send()
        for stage in range(2):
            for copy in stage_copies(n, stage, False):
                copy.wait_send()


def combine(c_ref, d_ref, g_ref, r_ref, out_ref, res_ref):
    out_ref[0] = c_ref[0, 0] * d_ref[...].astype(F32) + c_ref[8, 0] * g_ref[...].astype(F32)
    res_ref[...] = r_ref[...]


def per_device(measured, angles, counts, bands, zfoot):
    vmem, smem = pl.BlockSpec(memory_space=pltpu.VMEM), pl.BlockSpec(memory_space=pltpu.SMEM)
    volume16, volume32 = pltpu.VMEM((ROWS, 128), BF16), pltpu.VMEM((ROWS, 128), F32)
    out_d, out_g, out_c, out_r = pl.pallas_call(
        kernel,
        out_shape=(
            jax.ShapeDtypeStruct((CZ, GRID * GRID), BF16),
            jax.ShapeDtypeStruct((CZ, GRID * GRID), BF16),
            jax.ShapeDtypeStruct((16, 128), F32),
            jax.ShapeDtypeStruct((1, OWN, BAND, 128), F32),
        ),
        in_specs=[pl.BlockSpec(memory_space=pl.ANY), vmem, vmem, smem, smem],
        out_specs=(vmem,) * 4,
        scratch_shapes=[
            pltpu.VMEM((2, 8, 128), jnp.int32),
            pltpu.VMEM((2 * KS * JS, 128), jnp.int32),
            pltpu.SMEM((2 * KS * JS, 128), jnp.int32),
            pltpu.VMEM((KS, JS * LANES), F32),
            pltpu.VMEM((SIDE, LANES), F32),
            pltpu.VMEM((SIDE, LANES), F32),
            pltpu.VMEM((BAND, 128), BF16),
            pltpu.VMEM((PER * (BAND + 32), PER * CZ), BF16),
            pltpu.VMEM((PER * BAND, PER * 32), BF16),
            pltpu.VMEM((PER * BAND, PER * 48), BF16),
            pltpu.VMEM((PER * BAND, 128), F32),
            pltpu.VMEM((KS, 256, JS * LANES), BF16),
            pltpu.VMEM((KS, 128, 256), BF16),
            pltpu.VMEM((KS * JS, CZ, 256), F32),
            pltpu.VMEM((KS * JS, CZ, 128), F32),
            pltpu.VMEM((KS * JS, CZ, 256), F32),
            pltpu.VMEM((JS * LANES, 128), BF16),
            pltpu.VMEM((JS * LANES, 128), BF16),
            pltpu.VMEM((POS * 128, 128), F32),
            pltpu.VMEM((POS, 48, 128), BF16),
            pltpu.VMEM((TILES, PER * BAND, 128), F32),
            volume32, volume32, volume32, volume16, volume16,
            pltpu.VMEM((2, ROWS, 128), BF16),
            volume16, volume16, volume16,
            pltpu.VMEM((TILES, PER * CZ, 128), F32),
            pltpu.VMEM((2, TILES, PER * CZ, 128), BF16),
            pltpu.VMEM((2, TILES, PER * CZ, 128), BF16),
            pltpu.VMEM((TILES, PER * BAND, 128), F32),
            pltpu.VMEM((2, TILES, PER * BAND, 128), F32),
            pltpu.VMEM((2, TILES, PER * 32, 128), BF16),
            pltpu.VMEM((2, TILES, PER * 32, 128), BF16),
            pltpu.VMEM((2, 8, 8, 128), F32),
            pltpu.VMEM((2, 16, 8, 128), F32),
            pltpu.SemaphoreType.DMA((3,)),
            pltpu.SemaphoreType.DMA((5,)),
            pltpu.SemaphoreType.DMA((2, KS // 2)),
            pltpu.SemaphoreType.DMA((2, KS // 2)),
            pltpu.SemaphoreType.DMA((4,)),
            pltpu.SemaphoreType.DMA((4,)),
            pltpu.SemaphoreType.DMA((2, TILES)),
            pltpu.SemaphoreType.DMA((2, TILES)),
            pltpu.SemaphoreType.DMA((2, TILES, 2)),
            pltpu.SemaphoreType.DMA((2, TILES, 2)),
            pltpu.SemaphoreType.DMA((2, 24)),
            pltpu.SemaphoreType.DMA((2, 24)),
        ],
        compiler_params=pltpu.CompilerParams(
            collective_id=0, has_side_effects=True, vmem_limit_bytes=60 * 1024 * 1024
        ),
    )(measured, angles, zfoot, counts, bands)
    chunk = 8192
    half = pl.BlockSpec((CZ, chunk), lambda i: (0, i))
    rows = pl.BlockSpec((1, OWN, BAND, 128), lambda i: (0, 0, 0, 0))
    return pl.pallas_call(
        combine,
        grid=(GRID * GRID // chunk,),
        out_shape=(
            jax.ShapeDtypeStruct((1, CZ, GRID * GRID), F32),
            jax.ShapeDtypeStruct((1, OWN, BAND, 128), F32),
        ),
        in_specs=[smem, half, half, rows],
        out_specs=(pl.BlockSpec((1, CZ, chunk), lambda i: (0, 0, i)), rows),
    )(out_c, out_d, out_g, out_r)


def solution(mesh):
    placed = (P("phase", "angle", None, None), P("phase", "angle"), P(), P(), P("slab", None))
    return jax.shard_map(
        per_device,
        mesh=mesh,
        in_specs=placed,
        out_specs=(P("phase", "slab", None), P("phase", "angle", "slab", None)),
        check_vma=False,
    )
```
